32 devices in a mesh: row: 4 (over y, x), col: 8 (over z, core).
Axes of the slice: x: 2, y: 2, z: 4, core: 2. Of those that a mesh axis runs over, the one named last changes fastest.
Arguments:
- features: bfloat16 [16384, 128], P(('col', 'row')), may hold values from -6 to 6
- weight: bfloat16 [128, 256], replicated, may hold values from -0.5 to 0.5
- out_grad: bfloat16 [16384, 256], P(('row', 'col')), may hold values from -0.796875 to 0.796875
- tile_index: int32 [4, 8, 64, 3], P('row', 'col'), may hold values from 0 to 31, as said below
- edge_mask: int32 [4, 8, 64, 128, 128], P('row', 'col'), may hold values 0 or 1
- edge_weight: bfloat16 [4, 8, 64, 128, 128], P('row', 'col'), may hold values from 0 to 1
Outputs:
- edge_grad: bfloat16 [4, 8, 64, 128, 128], P('row', 'col')
- feature_grad: bfloat16 [16384, 128], P(('col', 'row'))
The draws below stay inside these ranges and needn't reach their ends.
Inputs may be any that keep to these rules, and one draw needn't show every extreme that they name: `tile_index`: within one device the (tile row, tile column) pairs are distinct; tile rows lie below 32, tile columns below 16; live slots come first, a device has between 21 and 64 of them, and some device has all 64 live.
All inputs are finite; a program needn't handle non-finite values. No bound on the sum of `edge_mask` on one device may be relied on, other than what follows from the above.
Results may differ from the reference program's by a relative error of at most 0.0049.
Values may be sent and summed in bfloat16 or wider, within the bound.
No kernel may reach another device: no remote copies, remote signals or barrier semaphores. Data moves between devices by JAX's collectives and lax.ppermute only.
A program may use at most 64 MiB of HBM per device.

```python
import jax
import jax.numpy as jnp
from jax import lax

F = 256
FIN = 128
BLOCK = 128
NODE_DEV = 512
TILES_DEV = 64
NODES = 16384
RB = 32
CB = 16
N_ROW = 4
N_COL = 8


def draw_tile_index(key, part):
    devices = N_ROW * N_COL
    cells = RB * CB
    keys = jax.random.split(jax.random.fold_in(key, 11), devices)
    picks = jax.vmap(lambda sub: jax.random.permutation(sub, cells)[:TILES_DEV])(keys).astype(jnp.int32)
    counts = jax.random.randint(jax.random.fold_in(key, 12), (devices,), TILES_DEV // 3, TILES_DEV + 1)
    fullest = jax.random.randint(jax.random.fold_in(key, 13), (), 0, devices)
    counts = jnp.where(jnp.arange(devices) == fullest, TILES_DEV, counts)
    inner = (jax.random.permutation(jax.random.fold_in(key, 14), cells - 2)[:TILES_DEV - 2] + 1).astype(jnp.int32)
    special = jnp.concatenate([jnp.array([cells - 1, 0], jnp.int32), inner])
    picks = jnp.where((jnp.arange(devices) == fullest)[:, None], special[None, :], picks)
    live = (jnp.arange(TILES_DEV)[None, :] < counts[:, None]).astype(jnp.int32)
    table = jnp.stack([picks // CB, picks % CB, live], axis=-1)
    return table.reshape(N_ROW, N_COL, TILES_DEV, 3).astype(jnp.int32)


def touch_ends(drawn, rng, least, largest):
    extent = drawn.shape
    index_at = [jax.random.randint(jax.random.fold_in(rng, axis), (), 0, extent[axis]) for axis in range(len(extent))]
    drawn = drawn.at[tuple(index_at)].set(least)
    longest = extent.index(max(extent))
    index_at[longest] = (index_at[longest] + 1) % extent[longest]
    return drawn.at[tuple(index_at)].set(largest)


def shard_levels(own_key, shape, cuts, low, high):
    def one(position, shards_of):
        draws = jax.random.uniform(jax.random.fold_in(jax.random.fold_in(own_key, 6), position), (shards_of,), jnp.float32, low / len(cuts), high / len(cuts))
        return jnp.repeat(jnp.exp(draws), shape[position] // shards_of).reshape((-1,) + (1,) * (len(shape) - position - 1))

    factor_of = one(*cuts[0])
    for cut in cuts[1:]:
        factor_of = factor_of * one(*cut)
    return factor_of


def gaussian(rng, extent, spread, most, pieces=(), held_as=jnp.bfloat16):
    drawn = spread * jax.random.normal(rng, extent, jnp.float32)
    if pieces:
        drawn = drawn * shard_levels(rng, extent, pieces, -0.22, 0.18)
    return jnp.clip(drawn, -most, most).astype(held_as)


def setup_inputs(seed: int = 0) -> dict:
    arg_keys = jax.random.split(jax.random.key(seed), 7)
    return {
        "features": gaussian(arg_keys[0], (NODES, FIN), 1.0, 6.0, ((0, 32),)),
        "weight": gaussian(arg_keys[1], (FIN, F), FIN ** -0.5, 0.5),
        "out_grad": gaussian(arg_keys[2], (NODES, F), 0.1, 0.796875, ((0, 32),)),
        "tile_index": draw_tile_index(jax.random.fold_in(arg_keys[6], 71), 0),
        "edge_mask": touch_ends((jax.random.randint(arg_keys[4], (N_ROW, N_COL, TILES_DEV, BLOCK, BLOCK), 0, 4) < 1).astype(jnp.int32), jax.random.fold_in(arg_keys[4], 1), 0, 1),
        "edge_weight": jnp.clip(1.0 * jax.random.uniform(arg_keys[5], (N_ROW, N_COL, TILES_DEV, BLOCK, BLOCK), jnp.float32) ** shard_levels(arg_keys[5], (N_ROW, N_COL, TILES_DEV, BLOCK, BLOCK), ((0, 4), (1, 8)), -0.2, 0.2), 0.0, 1.0).astype(jnp.bfloat16),
    }


def reference(features, weight, out_grad, tile_index, edge_mask, edge_weight):
    proj = jnp.dot(features, weight, preferred_element_type=jnp.float32).astype(jnp.bfloat16)
    row_panel = NODE_DEV * N_COL
    col_panel = NODE_DEV * N_ROW
    flat_index = tile_index.reshape(-1, 3).astype(jnp.int32)
    masks = edge_mask.reshape(-1, BLOCK, BLOCK)
    weights = edge_weight.reshape(-1, BLOCK, BLOCK)
    device = jnp.arange(flat_index.shape[0], dtype=jnp.int32) // TILES_DEV
    row_start = ((device // N_COL) * row_panel + flat_index[:, 0] * BLOCK).astype(jnp.int32)
    col_start = ((device % N_COL) * col_panel + flat_index[:, 1] * BLOCK).astype(jnp.int32)

    def step(total, item):
        rstart, cstart, live, mask_tile, weight_tile = item
        grad_rows = lax.dynamic_slice_in_dim(out_grad, rstart, BLOCK, 0)
        proj_cols = lax.dynamic_slice_in_dim(proj, cstart, BLOCK, 0)
        keep = mask_tile.astype(jnp.float32) * live.astype(jnp.float32)
        scores = jnp.dot(grad_rows, proj_cols.T, preferred_element_type=jnp.float32)
        grad_tile = (keep * scores).astype(jnp.bfloat16)
        adjacency = (weight_tile.astype(jnp.float32) * keep).astype(jnp.bfloat16)
        contrib = jnp.dot(adjacency.T, grad_rows, preferred_element_type=jnp.float32)
        current = lax.dynamic_slice_in_dim(total, cstart, BLOCK, 0)
        total = lax.dynamic_update_slice_in_dim(total, current + contrib, cstart, 0)
        return total, grad_tile

    start_total = jnp.zeros((features.shape[0], out_grad.shape[1]), jnp.float32)
    proj_grad, grads = lax.scan(step, start_total, (row_start, col_start, flat_index[:, 2], masks, weights))
    feature_grad = jnp.dot(proj_grad, weight.astype(jnp.float32).T, precision=lax.Precision.HIGHEST)
    return grads.reshape(edge_mask.shape), feature_grad.astype(jnp.bfloat16)
```

```python
import functools

import jax
import jax.numpy as jnp
from jax import lax
from jax.experimental import pallas as pl
from jax.experimental.pallas import tpu as pltpu
from jax.sharding import PartitionSpec as P

BLOCK = 128
GROUP = 8
VMEM = pltpu.VMEM
SMEM = pltpu.SMEM


def swap(x, axis, size, mask):
    return lax.ppermute(x, axis, [(i, i ^ mask) for i in range(size)])


def prep_kernel(table, mask, weights, keep_out, adj_out):
    step = pl.program_id(0)
    for i in range(GROUP):
        t = step * GROUP + i
        live = table[0, 0, t, 2]
        on = mask[0, 0, i] * live != 0
        adj = jnp.where(on, weights[0, 0, i].astype(jnp.float32), 0.0)
        keep_out[t] = jnp.where(on, 1.0, 0.0).astype(jnp.bfloat16)
        adj_out[t] = adj.T.astype(jnp.bfloat16)


def sums_kernel(n_row, n_col, per, *refs):
    table, adj = refs[:2]
    slots = refs[2 : 2 + n_col]
    panel = refs[2 + n_col]
    outs = refs[3 + n_col : 3 + n_col + n_row]
    total = refs[3 + n_col + n_row]
    me = lax.axis_index("col")
    row = lax.axis_index("row")
    for s in range(n_col):
        for i in range(per):
            panel[s * per + i] = slots[s][i * BLOCK : (i + 1) * BLOCK, :]
    total[...] = jnp.zeros_like(total)

    def group(step, carry):
        found = []
        for i in range(GROUP):
            t = step * GROUP + i
            a = table[0, 0, t, 0]
            place = ((a // per) ^ me) * per + a % per
            found.append(
                jnp.dot(adj[t], panel[place], preferred_element_type=jnp.float32)
            )
        for i in range(GROUP):
            b = table[0, 0, step * GROUP + i, 1]
            total[b] += found[i]
        return carry

    lax.fori_loop(0, adj.shape[0] // GROUP, group, 0)
    for s in range(n_row):
        for i in range(per):
            outs[s][i * BLOCK : (i + 1) * BLOCK, :] = total[(row ^ s) * per + i].astype(outs[s].dtype)


def scores_kernel(n_row, per, *refs):
    table, panel, keep = refs[:3]
    slots = refs[3 : 3 + n_row]
    out = refs[3 + n_row]
    cols = refs[4 + n_row]
    step = pl.program_id(0)
    me = lax.axis_index("col")
    row = lax.axis_index("row")

    @pl.when(step == 0)
    def _():
        for s in range(n_row):
            for i in range(per):
                block = slots[s][i * BLOCK : (i + 1) * BLOCK, :]
                cols[s * per + i] = block.astype(jnp.float32).T.astype(jnp.bfloat16)

    for i in range(GROUP):
        t = step * GROUP + i
        a = table[0, 0, t, 0]
        b = table[0, 0, t, 1]
        left = panel[((a // per) ^ me) * per + a % per]
        right = cols[((b // per) ^ row) * per + b % per]
        found = jnp.dot(left, right, preferred_element_type=jnp.float32)
        out[0, 0, i] = found.astype(jnp.bfloat16) * keep[t]


def local(n_row, n_col, features, weight, out_grad, tile_index, edge_mask, edge_weight):
    tiles = edge_mask.shape[2]
    nodes, fin = features.shape
    per = nodes // BLOCK
    whole = pl.BlockSpec(memory_space=VMEM)
    scalars = pl.BlockSpec(memory_space=SMEM)
    tile_block = pl.BlockSpec((1, 1, GROUP, BLOCK, BLOCK), lambda g: (0, 0, g, 0, 0))
    tile_set = jax.ShapeDtypeStruct((tiles, BLOCK, BLOCK), jnp.bfloat16)

    hidden = lax.dot_general(
        out_grad, weight, (((1,), (1,)), ((), ())), preferred_element_type=jnp.float32
    ).astype(jnp.bfloat16)

    slots = [None] * n_col
    slots[0] = hidden
    for s in range(2, n_col, 2):
        slots[s] = swap(hidden, "col", n_col, s)
    for s in range(0, n_col, 2):
        slots[s + 1] = swap(slots[s], "col", n_col, 1)
    col_slots = [features] + [swap(features, "row", n_row, s) for s in range(1, n_row)]

    keep, adj = pl.pallas_call(
        prep_kernel,
        grid=(tiles // GROUP,),
        in_specs=[scalars, tile_block, tile_block],
        out_specs=[whole, whole],
        out_shape=[tile_set, tile_set],
        cost_estimate=pl.CostEstimate(flops=0, bytes_accessed=edge_mask.size * 6, transcendentals=0),
        name="prep",
    )(tile_index, edge_mask, edge_weight)

    panel_shape = jax.ShapeDtypeStruct((n_col * per, BLOCK, fin), jnp.bfloat16)
    chunk = lambda dtype: jax.ShapeDtypeStruct((nodes, fin), dtype)
    panel, own, *parts = pl.pallas_call(
        functools.partial(sums_kernel, n_row, n_col, per),
        in_specs=[scalars] + [whole] * (1 + n_col),
        out_specs=[whole] * (1 + n_row),
        out_shape=[panel_shape, chunk(jnp.float32)] + [chunk(jnp.bfloat16)] * (n_row - 1),
        scratch_shapes=[VMEM((n_row * per, BLOCK, fin), jnp.float32)],
        cost_estimate=pl.CostEstimate(flops=2 * tiles * BLOCK * BLOCK * fin, bytes_accessed=4 << 20, transcendentals=0),
        name="sums",
    )(tile_index, adj, *slots)

    got = [swap(parts[s - 1], "row", n_row, s) for s in range(1, n_row)]

    edge_grad = pl.pallas_call(
        functools.partial(scores_kernel, n_row, per),
        grid=(tiles // GROUP,),
        in_specs=[scalars] + [whole] * (2 + n_row),
        out_specs=tile_block,
        out_shape=jax.ShapeDtypeStruct(edge_weight.shape, jnp.bfloat16),
        scratch_shapes=[VMEM((n_row * per, fin, BLOCK), jnp.bfloat16)],
        cost_estimate=pl.CostEstimate(flops=2 * tiles * BLOCK * BLOCK * fin, bytes_accessed=8 << 20, transcendentals=0),
        name="scores",
    )(tile_index, panel, keep, *col_slots)

    total = own
    for part in got:
        total = total + part.astype(jnp.float32)
    return edge_grad, total.astype(jnp.bfloat16)


def solution(mesh):
    in_specs = (
        P(("col", "row"), None),
        P(),
        P(("row", "col"), None),
        P("row", "col", None, None),
        P("row", "col", None, None, None),
        P("row", "col", None, None, None),
    )
    out_specs = (P("row", "col", None, None, None), P(("col", "row"), None))
    step = functools.partial(local, mesh.shape["row"], mesh.shape["col"])
    return jax.shard_map(step, mesh=mesh, in_specs=in_specs, out_specs=out_specs, check_vma=False)
```

```python
import functools

import jax
import jax.numpy as jnp
from jax import lax
from jax.experimental import pallas as pl
from jax.experimental.pallas import tpu as pltpu
from jax.sharding import PartitionSpec as P

BLOCK = 128
GROUP = 8
KERNEL_VMEM = 24 << 20
VMEM = pltpu.VMEM
SMEM = pltpu.SMEM


def swap(x, axis, size, mask):
    return lax.ppermute(x, axis, [(i, i ^ mask) for i in range(size)])


def in_vmem(x):
    return pltpu.with_memory_space_constraint(x, VMEM)


def prep_kernel(table, mask, weights, keep_out, adj_out):
    step = pl.program_id(0)
    for i in range(GROUP):
        t = step * GROUP + i
        live = table[0, 0, t, 2]
        on = mask[0, 0, i] * live != 0
        adj = jnp.where(on, weights[0, 0, i].astype(jnp.float32), 0.0)
        keep_out[t] = jnp.where(on, 1.0, 0.0).astype(jnp.bfloat16)
        adj_out[t] = adj.T.astype(jnp.bfloat16)


def sums_kernel(n_row, n_col, per, *refs):
    table, adj = refs[:2]
    slots = refs[2 : 2 + n_col]
    panel = refs[2 + n_col]
    outs = refs[3 + n_col : 3 + n_col + n_row]
    total = refs[3 + n_col + n_row]
    me = lax.axis_index("col")
    row = lax.axis_index("row")
    for s in range(n_col):
        for i in range(per):
            panel[s * per + i] = slots[s][i * BLOCK : (i + 1) * BLOCK, :]
    total[...] = jnp.zeros_like(total)

    def group(step, carry):
        found = []
        for i in range(GROUP):
            t = step * GROUP + i
            a = table[0, 0, t, 0]
            place = ((a // per) ^ me) * per + a % per
            found.append(
                jnp.dot(adj[t], panel[place], preferred_element_type=jnp.float32)
            )
        for i in range(GROUP):
            b = table[0, 0, step * GROUP + i, 1]
            total[b] += found[i]
        return carry

    lax.fori_loop(0, adj.shape[0] // GROUP, group, 0)
    for s in range(n_row):
        for i in range(per):
            outs[s][i * BLOCK : (i + 1) * BLOCK, :] = total[(row ^ s) * per + i].astype(outs[s].dtype)


def scores_kernel(n_row, per, *refs):
    table, panel, keep = refs[:3]
    slots = refs[3 : 3 + n_row]
    out = refs[3 + n_row]
    cols = refs[4 + n_row]
    step = pl.program_id(0)
    me = lax.axis_index("col")
    row = lax.axis_index("row")

    @pl.when(step == 0)
    def _():
        for s in range(n_row):
            for i in range(per):
                block = slots[s][i * BLOCK : (i + 1) * BLOCK, :]
                cols[s * per + i] = block.astype(jnp.float32).T.astype(jnp.bfloat16)

    for i in range(GROUP):
        t = step * GROUP + i
        a = table[0, 0, t, 0]
        b = table[0, 0, t, 1]
        left = panel[((a // per) ^ me) * per + a % per]
        right = cols[((b // per) ^ row) * per + b % per]
        found = jnp.dot(left, right, preferred_element_type=jnp.float32)
        out[0, 0, i] = found.astype(jnp.bfloat16) * keep[t]


def local(n_row, n_col, features, weight, out_grad, tile_index, edge_mask, edge_weight):
    tiles = edge_mask.shape[2]
    nodes, fin = features.shape
    per = nodes // BLOCK
    whole = pl.BlockSpec(memory_space=VMEM)
    scalars = pl.BlockSpec(memory_space=SMEM)
    tile_block = pl.BlockSpec((1, 1, GROUP, BLOCK, BLOCK), lambda g: (0, 0, g, 0, 0))
    tile_set = VMEM((tiles, BLOCK, BLOCK), jnp.bfloat16)

    hidden = lax.dot_general(
        out_grad, weight, (((1,), (1,)), ((), ())), preferred_element_type=jnp.float32
    ).astype(jnp.bfloat16)

    near = [swap(hidden, "col", n_col, s) for s in range(2, n_col, 2)]
    features, hidden = lax.optimization_barrier((features, hidden))
    cols = [swap(features, "row", n_row, s) for s in range(1, n_row)]

    keep, adj = pl.pallas_call(
        prep_kernel,
        grid=(tiles // GROUP,),
        in_specs=[scalars, tile_block, tile_block],
        out_specs=[whole, whole],
        out_shape=[tile_set, tile_set],
        cost_estimate=pl.CostEstimate(flops=0, bytes_accessed=edge_mask.size * 6, transcendentals=0),
        compiler_params=pltpu.CompilerParams(vmem_limit_bytes=KERNEL_VMEM),
        name="prep",
    )(tile_index, edge_mask, edge_weight)

    near, cols, keep, adj = lax.optimization_barrier((near, cols, keep, adj))
    slots = [None] * n_col
    slots[::2] = [hidden] + near
    slots[1::2] = [swap(x, "col", n_col, 1) for x in slots[::2]]
    col_slots = [features] + cols

    panel_shape = VMEM((n_col * per, BLOCK, fin), jnp.bfloat16)
    chunk = lambda dtype: VMEM((nodes, fin), dtype)
    panel, own, *parts = pl.pallas_call(
        functools.partial(sums_kernel, n_row, n_col, per),
        in_specs=[scalars] + [whole] * (1 + n_col),
        out_specs=[whole] * (1 + n_row),
        out_shape=[panel_shape, chunk(jnp.float32)] + [chunk(jnp.bfloat16)] * (n_row - 1),
        scratch_shapes=[VMEM((n_row * per, BLOCK, fin), jnp.float32)],
        cost_estimate=pl.CostEstimate(flops=2 * tiles * BLOCK * BLOCK * fin, bytes_accessed=4 << 20, transcendentals=0),
        compiler_params=pltpu.CompilerParams(vmem_limit_bytes=KERNEL_VMEM),
        name="sums",
    )(tile_index, *map(in_vmem, (adj, *slots)))

    got = [swap(parts[s - 1], "row", n_row, s) for s in range(1, n_row)]

    edge_grad = pl.pallas_call(
        functools.partial(scores_kernel, n_row, per),
        grid=(tiles // GROUP,),
        in_specs=[scalars] + [whole] * (2 + n_row),
        out_specs=tile_block,
        out_shape=jax.ShapeDtypeStruct(edge_weight.shape, jnp.bfloat16),
        scratch_shapes=[VMEM((n_row * per, fin, BLOCK), jnp.bfloat16)],
        cost_estimate=pl.CostEstimate(flops=2 * tiles * BLOCK * BLOCK * fin, bytes_accessed=8 << 20, transcendentals=0),
        compiler_params=pltpu.CompilerParams(vmem_limit_bytes=KERNEL_VMEM),
        name="scores",
    )(tile_index, *map(in_vmem, (panel, keep, *col_slots)))

    total = own
    for part in got:
        total = total + part.astype(jnp.float32)
    return edge_grad, total.astype(jnp.bfloat16)


def solution(mesh):
    in_specs = (
        P(("col", "row"), None),
        P(),
        P(("row", "col"), None),
        P("row", "col", None, None),
        P("row", "col", None, None, None),
        P("row", "col", None, None, None),
    )
    out_specs = (P("row", "col", None, None, None), P(("col", "row"), None))
    step = functools.partial(local, mesh.shape["row"], mesh.shape["col"])
    return jax.shard_map(step, mesh=mesh, in_specs=in_specs, out_specs=out_specs, check_vma=False)
```

```python
import functools

import jax
import jax.numpy as jnp
from jax import lax
from jax.experimental import pallas as pl
from jax.experimental.pallas import tpu as pltpu
from jax.sharding import PartitionSpec as P

BLOCK = 128
GROUP = 8
KERNEL_VMEM = 24 << 20
VMEM = pltpu.VMEM
SMEM = pltpu.SMEM


def in_vmem(x):
    return pltpu.with_memory_space_constraint(x, VMEM)


def in_hbm(x):
    return pltpu.with_memory_space_constraint(x, pltpu.HBM)


def swap(x, axis, size, mask):
    return lax.ppermute(x, axis, [(i, i ^ mask) for i in range(size)])


def prep_kernel(n_row, n_col, per, index, mask, weights, keep_out, adj_out, places, table, mask_buf, weight_buf, sems, table_sem):
    tiles = mask_buf.shape[0]
    groups = tiles // GROUP
    me = lax.axis_index("col")
    row = lax.axis_index("row")

    def fetch(g):
        span = pl.ds(pl.multiple_of(g * GROUP, GROUP), GROUP)
        return (
            pltpu.make_async_copy(mask.at[0, 0, span], mask_buf.at[span], sems.at[0, g]),
            pltpu.make_async_copy(weights.at[0, 0, span], weight_buf.at[span], sems.at[1, g]),
        )

    table_copy = pltpu.make_async_copy(index, table, table_sem)
    table_copy.start()
    for g in range(groups):
        for copy in fetch(g):
            copy.start()
    table_copy.wait()

    def body(g, carry):
        for i in range(GROUP):
            t = g * GROUP + i
            a = table[0, 0, 0, t]
            b = table[0, 1, 0, t]
            places[t] = ((a // per) ^ me) * per + a % per
            places[tiles + t] = ((b // per) ^ row) * per + b % per
        for copy in fetch(g):
            copy.wait()
        for i in range(GROUP):
            t = g * GROUP + i
            keep = (mask_buf[t] * table[0, 2, 0, t]).astype(jnp.float32).astype(jnp.bfloat16)
            keep_out[t] = keep
            adj_out[t] = (weight_buf[t] * keep).T
        return carry

    lax.fori_loop(0, groups, body, 0)


def sums_kernel(n_row, n_col, per, *refs):
    places, adj = refs[:2]
    slots = refs[2 : 2 + n_col]
    panel = refs[2 + n_col]
    outs = refs[3 + n_col : 3 + n_col + n_row]
    total = refs[3 + n_col + n_row]
    tiles = adj.shape[0]
    for s in range(n_col):
        for i in range(per):
            panel[s * per + i] = slots[s][i * BLOCK : (i + 1) * BLOCK, :]
    total[...] = jnp.zeros_like(total)
    for t in range(tiles):
        total[places[tiles + t]] += jnp.dot(adj[t], panel[places[t]], preferred_element_type=jnp.float32)
    for s in range(n_row):
        for i in range(per):
            outs[s][i * BLOCK : (i + 1) * BLOCK, :] = total[s * per + i].astype(outs[s].dtype)


def scores_kernel(n_row, per, *refs):
    places, panel, keep = refs[:3]
    slots = refs[3 : 3 + n_row]
    out, cols, stage, sems = refs[3 + n_row :]
    tiles = keep.shape[0]
    for s in range(n_row):
        for i in range(per):
            cols[s * per + i] = slots[s][i * BLOCK : (i + 1) * BLOCK, :].T
    copies = []
    for g in range(tiles // GROUP):
        for t in range(g * GROUP, (g + 1) * GROUP):
            found = jnp.dot(panel[places[t]], cols[places[tiles + t]], preferred_element_type=jnp.float32)
            stage[t] = found.astype(jnp.bfloat16) * keep[t]
        span = pl.ds(g * GROUP, GROUP)
        copies.append(pltpu.make_async_copy(stage.at[span], out.at[0, 0, span], sems.at[g]))
        copies[-1].start()
    for copy in copies:
        copy.wait()


def local(n_row, n_col, features, weight, out_grad, tile_index, edge_mask, edge_weight):
    tiles = edge_mask.shape[2]
    nodes, fin = features.shape
    per = nodes // BLOCK
    whole = pl.BlockSpec(memory_space=VMEM)
    far = pl.BlockSpec(memory_space=pl.ANY)
    scalars = pl.BlockSpec(memory_space=SMEM)
    params = pltpu.CompilerParams(vmem_limit_bytes=KERNEL_VMEM)
    tile_set = VMEM((tiles, BLOCK, BLOCK), jnp.bfloat16)
    product_flops = 2 * tiles * BLOCK * BLOCK * fin

    hidden = lax.dot_general(
        out_grad, weight, (((1,), (1,)), ((), ())), preferred_element_type=jnp.float32
    ).astype(jnp.bfloat16)

    near = [swap(hidden, "col", n_col, s) for s in range(2, n_col, 2)]
    beside = swap(hidden, "col", n_col, 1)
    features, hidden = lax.optimization_barrier((features, hidden))
    cols = [swap(features, "row", n_row, s) for s in range(1, n_row)]

    index = jnp.transpose(tile_index, (0, 3, 1, 2))
    index, beside = lax.optimization_barrier((index, beside))
    keep, adj, places = pl.pallas_call(
        functools.partial(prep_kernel, n_row, n_col, per),
        in_specs=[far, far, far],
        out_specs=[whole, whole, scalars],
        out_shape=[tile_set, tile_set, SMEM((2 * tiles,), jnp.int32)],
        scratch_shapes=[
            SMEM(index.shape, jnp.int32),
            VMEM((tiles, BLOCK, BLOCK), jnp.int32),
            VMEM((tiles, BLOCK, BLOCK), jnp.bfloat16),
            pltpu.SemaphoreType.DMA((2, tiles // GROUP)),
            pltpu.SemaphoreType.DMA,
        ],
        cost_estimate=pl.CostEstimate(flops=0, bytes_accessed=6 * tiles * BLOCK * BLOCK, transcendentals=0),
        compiler_params=params,
        name="prep",
    )(index, in_hbm(edge_mask), in_hbm(edge_weight))
    places = pltpu.with_memory_space_constraint(places, SMEM)

    near, keep, adj = lax.optimization_barrier((near, keep, adj))
    slots = [None] * n_col
    slots[::2] = [hidden] + near
    slots[1::2] = [beside] + [swap(x, "col", n_col, 1) for x in near]
    slots, cols = lax.optimization_barrier((slots, cols))
    cols = [features] + cols

    panel, own, *parts = pl.pallas_call(
        functools.partial(sums_kernel, n_row, n_col, per),
        in_specs=[scalars] + [whole] * (1 + n_col),
        out_specs=[whole] * (1 + n_row),
        out_shape=[VMEM((n_col * per, BLOCK, fin), jnp.bfloat16), VMEM((nodes, fin), jnp.float32)]
        + [VMEM((nodes, fin), jnp.bfloat16)] * (n_row - 1),
        scratch_shapes=[VMEM((n_row * per, BLOCK, fin), jnp.float32)],
        cost_estimate=pl.CostEstimate(flops=product_flops, bytes_accessed=4 << 20, transcendentals=0),
        compiler_params=params,
        name="sums",
    )(places, *map(in_vmem, (adj, *slots)))

    got = [swap(part, "row", n_row, s + 1) for s, part in enumerate(parts)]

    edge_grad = pl.pallas_call(
        functools.partial(scores_kernel, n_row, per),
        in_specs=[scalars] + [whole] * (2 + n_row),
        out_specs=far,
        out_shape=jax.ShapeDtypeStruct(edge_weight.shape, jnp.bfloat16),
        scratch_shapes=[
            VMEM((n_row * per, fin, BLOCK), jnp.bfloat16),
            VMEM((tiles, BLOCK, BLOCK), jnp.bfloat16),
            pltpu.SemaphoreType.DMA((tiles // GROUP,)),
        ],
        cost_estimate=pl.CostEstimate(flops=product_flops, bytes_accessed=4 << 20, transcendentals=0),
        compiler_params=params,
        name="scores",
    )(places, *map(in_vmem, (panel, keep, *cols)))

    total = own
    for part in got:
        total = total + part.astype(jnp.float32)
    return edge_grad, total.astype(jnp.bfloat16)


def solution(mesh):
    in_specs = (
        P(("col", "row"), None),
        P(),
        P(("row", "col"), None),
        P("row", "col", None, None),
        P("row", "col", None, None, None),
        P("row", "col", None, None, None),
    )
    out_specs = (P("row", "col", None, None, None), P(("col", "row"), None))
    step = functools.partial(local, mesh.shape["row"], mesh.shape["col"])
    return jax.shard_map(step, mesh=mesh, in_specs=in_specs, out_specs=out_specs, check_vma=False)
```

```python
import functools

import jax
import jax.numpy as jnp
from jax import lax
from jax.experimental import pallas as pl
from jax.experimental.pallas import tpu as pltpu
from jax.sharding import PartitionSpec as P

BLOCK = 128
GROUP = 8
KERNEL_VMEM = 24 << 20
VMEM = pltpu.VMEM
SMEM = pltpu.SMEM


def in_vmem(x):
    return pltpu.with_memory_space_constraint(x, VMEM)


def in_hbm(x):
    return pltpu.with_memory_space_constraint(x, pltpu.HBM)


def swap(x, axis, size, mask):
    return lax.ppermute(x, axis, [(i, i ^ mask) for i in range(size)])


def swap_rows(x, n_row, n_col, even, odd):
    places = [(r, c) for r in range(n_row) for c in range(n_col)]
    pairs = [(r * n_col + c, (r ^ (odd if c % 2 else even)) * n_col + c) for r, c in places]
    return lax.ppermute(x, ("row", "col"), pairs)


def hidden_kernel(grads, weight, out, grad_buf, weight_buf, sems):
    copies = [
        pltpu.make_async_copy(grads, grad_buf, sems.at[0]),
        pltpu.make_async_copy(weight, weight_buf, sems.at[1]),
    ]
    for copy in copies:
        copy.start()
    for copy in copies:
        copy.wait()
    out[...] = lax.dot_general(
        grad_buf[...], weight_buf[...], (((1,), (1,)), ((), ())), preferred_element_type=jnp.float32
    ).astype(out.dtype)


def prep_kernel(n_row, n_col, per, index, mask, weights, keep_out, adj_out, places, table, mask_buf, weight_buf, sems, table_sem):
    tiles = mask_buf.shape[0]
    groups = tiles // GROUP
    me = lax.axis_index("col")
    row = lax.axis_index("row")
    core = me % 2
    bits = n_row.bit_length() - 1

    def fetch(g):
        span = pl.ds(pl.multiple_of(g * GROUP, GROUP), GROUP)
        return (
            pltpu.make_async_copy(mask.at[0, 0, span], mask_buf.at[span], sems.at[0, g]),
            pltpu.make_async_copy(weights.at[0, 0, span], weight_buf.at[span], sems.at[1, g]),
        )

    table_copy = pltpu.make_async_copy(index, table, table_sem)
    table_copy.start()
    for g in range(groups):
        for copy in fetch(g):
            copy.start()
    table_copy.wait()

    def body(g, carry):
        for i in range(GROUP):
            t = g * GROUP + i
            a = table[0, 0, 0, t]
            b = table[0, 1, 0, t]
            places[t] = ((a // per) ^ me) * per + a % per
            off = (b // per) ^ row
            back = sum(((off >> i) & 1) << (bits - 1 - i) for i in range(bits))
            places[tiles + t] = off * per + b % per
            places[2 * tiles + t] = (off + core * (back - off)) * per + b % per
        for copy in fetch(g):
            copy.wait()
        for i in range(GROUP):
            t = g * GROUP + i
            keep = (mask_buf[t] * table[0, 2, 0, t]).astype(jnp.float32).astype(jnp.bfloat16)
            keep_out[t] = keep
            adj_out[t] = (weight_buf[t] * keep).T
        return carry

    lax.fori_loop(0, groups, body, 0)


def sums_kernel(n_row, n_col, per, *refs):
    places, adj = refs[:2]
    slots = refs[2 : 2 + n_col]
    panel = refs[2 + n_col]
    outs = refs[3 + n_col : 3 + n_col + n_row]
    total = refs[3 + n_col + n_row]
    tiles = adj.shape[0]
    for s in range(n_col):
        for i in range(per):
            panel[s * per + i] = slots[s][i * BLOCK : (i + 1) * BLOCK, :]
    total[...] = jnp.zeros_like(total)
    for t in range(tiles):
        total[places[tiles + t]] += jnp.dot(adj[t], panel[places[t]], preferred_element_type=jnp.float32)
    for s in range(n_row):
        for i in range(per):
            outs[s][i * BLOCK : (i + 1) * BLOCK, :] = total[s * per + i].astype(outs[s].dtype)


def scores_kernel(places, panel, keep, features, out, cols, stage, sems):
    tiles = keep.shape[0]
    for i in range(cols.shape[0]):
        cols[i] = features[i * BLOCK : (i + 1) * BLOCK, :].T
    copies = []
    for g in range(tiles // GROUP):
        for t in range(g * GROUP, (g + 1) * GROUP):
            found = jnp.dot(panel[places[t]], cols[places[2 * tiles + t]], preferred_element_type=jnp.float32)
            stage[t] = found.astype(jnp.bfloat16) * keep[t]
        span = pl.ds(g * GROUP, GROUP)
        copies.append(pltpu.make_async_copy(stage.at[span], out.at[0, 0, span], sems.at[g]))
        copies[-1].start()
    for copy in copies:
        copy.wait()


def local(n_row, n_col, features, weight, out_grad, tile_index, edge_mask, edge_weight):
    tiles = edge_mask.shape[2]
    nodes, fin = features.shape
    per = nodes // BLOCK
    whole = pl.BlockSpec(memory_space=VMEM)
    far = pl.BlockSpec(memory_space=pl.ANY)
    scalars = pl.BlockSpec(memory_space=SMEM)
    params = pltpu.CompilerParams(vmem_limit_bytes=KERNEL_VMEM)
    tile_set = VMEM((tiles, BLOCK, BLOCK), jnp.bfloat16)
    product_flops = 2 * tiles * BLOCK * BLOCK * fin

    hidden = pl.pallas_call(
        hidden_kernel,
        in_specs=[far, far],
        out_specs=whole,
        out_shape=VMEM((nodes, fin), jnp.bfloat16),
        scratch_shapes=[
            VMEM(out_grad.shape, out_grad.dtype),
            VMEM(weight.shape, weight.dtype),
            pltpu.SemaphoreType.DMA((2,)),
        ],
        compiler_params=params,
        name="hidden",
    )(in_hbm(out_grad), in_hbm(weight))

    masks = [1 << i for i in reversed(range(1, n_col.bit_length() - 1))]
    shards = {0: hidden}
    for mask in masks:
        shards[mask] = swap(hidden, "col", n_col, mask)
    features, hidden = lax.optimization_barrier((features, hidden))
    bits = [1 << i for i in range(n_row.bit_length() - 1)]
    stages = list(zip(bits, reversed(bits), strict=True))
    cols = [features, swap_rows(features, n_row, n_col, *stages[0])]

    index = jnp.transpose(tile_index, (0, 3, 1, 2))
    keep, adj, places = pl.pallas_call(
        functools.partial(prep_kernel, n_row, n_col, per),
        in_specs=[far, far, far],
        out_specs=[whole, whole, scalars],
        out_shape=[tile_set, tile_set, SMEM((3 * tiles,), jnp.int32)],
        scratch_shapes=[
            SMEM(index.shape, jnp.int32),
            VMEM((tiles, BLOCK, BLOCK), jnp.int32),
            VMEM((tiles, BLOCK, BLOCK), jnp.bfloat16),
            pltpu.SemaphoreType.DMA((2, tiles // GROUP)),
            pltpu.SemaphoreType.DMA,
        ],
        cost_estimate=pl.CostEstimate(flops=0, bytes_accessed=4096, transcendentals=0),
        compiler_params=params,
        name="prep",
    )(in_hbm(index), in_hbm(edge_mask), in_hbm(edge_weight))
    places = pltpu.with_memory_space_constraint(places, SMEM)

    shards[masks[0]], hidden, keep, adj = lax.optimization_barrier((shards[masks[0]], hidden, keep, adj))
    shards[0] = hidden
    for i, mask in enumerate(masks[1:], 1):
        for s in range(masks[i - 1], n_col, masks[i - 1]):
            shards[s ^ mask] = swap(shards[s], "col", n_col, mask)
    cols = jnp.concatenate(cols)
    for stage in stages[1:]:
        cols = jnp.concatenate([cols, swap_rows(cols, n_row, n_col, *stage)])
    slots = [shards[s] for s in range(0, n_col, 2)]
    slots = [x for shard in slots for x in (shard, swap(shard, "col", n_col, 1))]

    panel, own, *parts = pl.pallas_call(
        functools.partial(sums_kernel, n_row, n_col, per),
        in_specs=[scalars] + [whole] * (1 + n_col),
        out_specs=[whole] * (1 + n_row),
        out_shape=[VMEM((n_col * per, BLOCK, fin), jnp.bfloat16), VMEM((nodes, fin), jnp.float32)]
        + [VMEM((nodes, fin), jnp.bfloat16)] * (n_row - 1),
        scratch_shapes=[VMEM((n_row * per, BLOCK, fin), jnp.float32)],
        cost_estimate=pl.CostEstimate(flops=0, bytes_accessed=4096, transcendentals=0),
        compiler_params=params,
        name="sums",
    )(places, *map(in_vmem, (adj, *slots)))

    order = sorted(range(1, n_row), key=lambda s: -s.bit_count())
    got = [swap(parts[s - 1], "row", n_row, s) for s in order]

    edge_grad = pl.pallas_call(
        scores_kernel,
        in_specs=[scalars] + [whole] * 3,
        out_specs=far,
        out_shape=jax.ShapeDtypeStruct(edge_weight.shape, jnp.bfloat16),
        scratch_shapes=[
            VMEM((n_row * per, fin, BLOCK), jnp.bfloat16),
            VMEM((tiles, BLOCK, BLOCK), jnp.bfloat16),
            pltpu.SemaphoreType.DMA((tiles // GROUP,)),
        ],
        cost_estimate=pl.CostEstimate(flops=product_flops, bytes_accessed=4 << 20, transcendentals=0),
        compiler_params=params,
        name="scores",
    )(places, *map(in_vmem, (panel, keep, cols)))

    total = own
    for part in got:
        total = total + part.astype(jnp.float32)
    return edge_grad, total.astype(jnp.bfloat16)


def solution(mesh):
    in_specs = (
        P(("col", "row"), None),
        P(),
        P(("row", "col"), None),
        P("row", "col", None, None),
        P("row", "col", None, None, None),
        P("row", "col", None, None, None),
    )
    out_specs = (P("row", "col", None, None, None), P(("col", "row"), None))
    step = functools.partial(local, mesh.shape["row"], mesh.shape["col"])
    return jax.shard_map(step, mesh=mesh, in_specs=in_specs, out_specs=out_specs, check_vma=False)
```

```python
import functools

import jax
import jax.numpy as jnp
from jax import lax
from jax.experimental import pallas as pl
from jax.experimental.pallas import tpu as pltpu
from jax.sharding import PartitionSpec as P

BLOCK = 128
GROUP = 8
KERNEL_VMEM = 24 << 20
VMEM = pltpu.VMEM
SMEM = pltpu.SMEM


def in_vmem(x):
    return pltpu.with_memory_space_constraint(x, VMEM)


def in_hbm(x):
    return pltpu.with_memory_space_constraint(x, pltpu.HBM)


def swap(x, axis, size, mask):
    return lax.ppermute(x, axis, [(i, i ^ mask) for i in range(size)])


def swap_rows(x, n_row, n_col, even, odd):
    places = [(r, c) for r in range(n_row) for c in range(n_col)]
    pairs = [(r * n_col + c, (r ^ (odd if c % 2 else even)) * n_col + c) for r, c in places]
    return lax.ppermute(x, ("row", "col"), pairs)


def hidden_kernel(grads, weight, out, grad_buf, weight_buf, sems):
    copies = [
        pltpu.make_async_copy(grads, grad_buf, sems.at[0]),
        pltpu.make_async_copy(weight, weight_buf, sems.at[1]),
    ]
    for copy in copies:
        copy.start()
    for copy in copies:
        copy.wait()
    out[...] = lax.dot_general(
        grad_buf[...], weight_buf[...], (((1,), (1,)), ((), ())), preferred_element_type=jnp.float32
    ).astype(out.dtype)


def prep_kernel(n_row, n_col, per, index, mask, weights, keep_out, adj_out, places, table, mask_buf, weight_buf, sems, table_sem):
    tiles = mask_buf.shape[0]
    groups = tiles // GROUP
    me = lax.axis_index("col")
    row = lax.axis_index("row")
    core = me % 2
    bits = n_row.bit_length() - 1

    def fetch(g):
        span = pl.ds(pl.multiple_of(g * GROUP, GROUP), GROUP)
        return (
            pltpu.make_async_copy(mask.at[0, 0, span], mask_buf.at[span], sems.at[0, g]),
            pltpu.make_async_copy(weights.at[0, 0, span], weight_buf.at[span], sems.at[1, g]),
        )

    table_copy = pltpu.make_async_copy(index, table, table_sem)
    table_copy.start()
    for g in range(groups):
        for copy in fetch(g):
            copy.start()
    table_copy.wait()

    def body(g, late):
        for i in range(GROUP):
            t = g * GROUP + i
            a = table[0, 0, 0, t]
            b = table[0, 1, 0, t]
            slot = (a // per) ^ me
            off = (b // per) ^ row
            back = sum(((off >> j) & 1) << (bits - 1 - j) for j in range(bits))
            places[t] = slot * per + a % per
            places[tiles + t] = (off + core * (back - off)) * per + b % per
            last = (slot == n_col - 1).astype(jnp.int32)
            at = (1 - last) * (t - late) + last * (tiles - 1 - late)
            late = late + last
            places[2 * tiles + at] = t
            places[3 * tiles + at] = off * per + b % per
            places[4 * tiles + at] = (1 - last) * per + last * (a % per)
        for copy in fetch(g):
            copy.wait()
        for i in range(GROUP):
            t = g * GROUP + i
            keep = (mask_buf[t] * table[0, 2, 0, t]).astype(jnp.float32).astype(jnp.bfloat16)
            keep_out[t] = keep
            adj_out[t] = (weight_buf[t] * keep).T
        return late

    late = lax.fori_loop(0, groups, body, jnp.int32(0))
    places[5 * tiles] = (tiles - late) // GROUP


def sums_kernel(per, *refs):
    places, adj, *slots, panel, total = refs
    tiles = adj.shape[0]
    for s, slot in enumerate(slots):
        for i in range(per):
            panel[s * per + i] = slot[i * BLOCK : (i + 1) * BLOCK, :]
    for i in range(len(slots) * per, panel.shape[0]):
        panel[i] = jnp.zeros_like(panel[i])
    total[...] = jnp.zeros_like(total)
    for p in range(tiles):
        t = places[2 * tiles + p]
        total[places[3 * tiles + p]] += jnp.dot(adj[t], panel[places[t]], preferred_element_type=jnp.float32)


def rest_kernel(per, places, adj, total, last, *refs):
    *outs, blocks, extra = refs
    tiles = adj.shape[0]
    for i in range(per):
        blocks[i] = last[i * BLOCK : (i + 1) * BLOCK, :]
    blocks[per] = jnp.zeros_like(blocks[per])
    extra[...] = jnp.zeros_like(extra)

    def body(g, carry):
        for i in range(GROUP):
            p = g * GROUP + i
            extra[places[3 * tiles + p]] += jnp.dot(
                adj[places[2 * tiles + p]], blocks[places[4 * tiles + p]], preferred_element_type=jnp.float32
            )
        return carry

    lax.fori_loop(places[5 * tiles], tiles // GROUP, body, 0)
    for s, out in enumerate(outs):
        for i in range(per):
            found = total[s * per + i] + extra[s * per + i]
            out[i * BLOCK : (i + 1) * BLOCK, :] = found.astype(out.dtype)


def scores_kernel(per, places, panel, last, keep, features, out, rows, cols, stage, sems):
    tiles = keep.shape[0]
    head = rows.shape[0] - per
    rows[:head] = panel[:head]
    for i in range(per):
        rows[head + i] = last[i * BLOCK : (i + 1) * BLOCK, :]
    for i in range(cols.shape[0]):
        cols[i] = features[i * BLOCK : (i + 1) * BLOCK, :].T
    copies = []
    for g in range(tiles // GROUP):
        for t in range(g * GROUP, (g + 1) * GROUP):
            found = jnp.dot(rows[places[t]], cols[places[tiles + t]], preferred_element_type=jnp.float32)
            stage[t] = found.astype(jnp.bfloat16) * keep[t]
        span = pl.ds(g * GROUP, GROUP)
        copies.append(pltpu.make_async_copy(stage.at[span], out.at[0, 0, span], sems.at[g]))
        copies[-1].start()
    for copy in copies:
        copy.wait()


def local(n_row, n_col, features, weight, out_grad, tile_index, edge_mask, edge_weight):
    tiles = edge_mask.shape[2]
    nodes, fin = features.shape
    per = nodes // BLOCK
    whole = pl.BlockSpec(memory_space=VMEM)
    far = pl.BlockSpec(memory_space=pl.ANY)
    scalars = pl.BlockSpec(memory_space=SMEM)
    params = pltpu.CompilerParams(vmem_limit_bytes=KERNEL_VMEM)
    tile_set = VMEM((tiles, BLOCK, BLOCK), jnp.bfloat16)
    product_flops = 2 * tiles * BLOCK * BLOCK * fin

    hidden = pl.pallas_call(
        hidden_kernel,
        in_specs=[far, far],
        out_specs=whole,
        out_shape=VMEM((nodes, fin), jnp.bfloat16),
        scratch_shapes=[
            VMEM(out_grad.shape, out_grad.dtype),
            VMEM(weight.shape, weight.dtype),
            pltpu.SemaphoreType.DMA((2,)),
        ],
        compiler_params=params,
        name="hidden",
    )(in_hbm(out_grad), in_hbm(weight))

    masks = [1 << i for i in reversed(range(1, n_col.bit_length() - 1))]
    shards = {0: hidden}
    for mask in masks:
        shards[mask] = swap(hidden, "col", n_col, mask)
    features, hidden = lax.optimization_barrier((features, hidden))
    bits = [1 << i for i in range(n_row.bit_length() - 1)]
    stages = list(zip(bits, reversed(bits), strict=True))
    cols = [features, swap_rows(features, n_row, n_col, *stages[0])]

    index = jnp.transpose(tile_index, (0, 3, 1, 2))
    keep, adj, places = pl.pallas_call(
        functools.partial(prep_kernel, n_row, n_col, per),
        in_specs=[far, far, far],
        out_specs=[whole, whole, scalars],
        out_shape=[tile_set, tile_set, SMEM((5 * tiles + 1,), jnp.int32)],
        scratch_shapes=[
            SMEM(index.shape, jnp.int32),
            VMEM((tiles, BLOCK, BLOCK), jnp.int32),
            VMEM((tiles, BLOCK, BLOCK), jnp.bfloat16),
            pltpu.SemaphoreType.DMA((2, tiles // GROUP)),
            pltpu.SemaphoreType.DMA,
        ],
        cost_estimate=pl.CostEstimate(flops=0, bytes_accessed=4096, transcendentals=0),
        compiler_params=params,
        name="prep",
    )(in_hbm(index), in_hbm(edge_mask), in_hbm(edge_weight))
    places = pltpu.with_memory_space_constraint(places, SMEM)

    shards[masks[0]], hidden, keep, adj = lax.optimization_barrier((shards[masks[0]], hidden, keep, adj))
    shards[0] = hidden
    cols, keep = lax.optimization_barrier((cols, keep))
    for i, mask in enumerate(masks[1:], 1):
        for s in range(masks[i - 1], n_col, masks[i - 1]):
            shards[s ^ mask] = swap(shards[s], "col", n_col, mask)
    cols = jnp.concatenate(cols)
    for stage in stages[1:]:
        cols = jnp.concatenate([cols, swap_rows(cols, n_row, n_col, *stage)])
    slots = [shards[s] for s in range(0, n_col, 2)]
    slots = [x for shard in slots for x in (shard, swap(shard, "col", n_col, 1))]

    *slots, last = slots
    total_shape = (n_row * per, BLOCK, fin)
    panel, total = pl.pallas_call(
        functools.partial(sums_kernel, per),
        in_specs=[scalars] + [whole] * n_col,
        out_specs=[whole] * 2,
        out_shape=[VMEM((n_col * per, BLOCK, fin), jnp.bfloat16), VMEM(total_shape, jnp.float32)],
        cost_estimate=pl.CostEstimate(flops=product_flops, bytes_accessed=1 << 20, transcendentals=0),
        compiler_params=params,
        name="sums",
    )(places, *map(in_vmem, (adj, *slots)))
    own, *parts = pl.pallas_call(
        functools.partial(rest_kernel, per),
        in_specs=[scalars] + [whole] * 3,
        out_specs=[whole] * n_row,
        out_shape=[VMEM((nodes, fin), jnp.float32)] + [VMEM((nodes, fin), jnp.bfloat16)] * (n_row - 1),
        scratch_shapes=[VMEM((per + 1, BLOCK, fin), jnp.bfloat16), VMEM(total_shape, jnp.float32)],
        cost_estimate=pl.CostEstimate(flops=0, bytes_accessed=4096, transcendentals=0),
        compiler_params=params,
        name="rest",
    )(places, *map(in_vmem, (adj, total, last)))

    order = sorted(range(1, n_row), key=lambda s: -s.bit_count())
    order = order[-1:] + order[:-1]
    got = [swap(parts[s - 1], "row", n_row, s) for s in order]

    edge_grad = pl.pallas_call(
        functools.partial(scores_kernel, per),
        in_specs=[scalars] + [whole] * 4,
        out_specs=far,
        out_shape=jax.ShapeDtypeStruct(edge_weight.shape, jnp.bfloat16),
        scratch_shapes=[
            VMEM((n_col * per, BLOCK, fin), jnp.bfloat16),
            VMEM((n_row * per, fin, BLOCK), jnp.bfloat16),
            VMEM((tiles, BLOCK, BLOCK), jnp.bfloat16),
            pltpu.SemaphoreType.DMA((tiles // GROUP,)),
        ],
        cost_estimate=pl.CostEstimate(flops=product_flops, bytes_accessed=4 << 20, transcendentals=0),
        compiler_params=params,
        name="scores",
    )(places, *map(in_vmem, (panel, last, keep, cols)))

    for part in got:
        own = own + part.astype(jnp.float32)
    return edge_grad, own.astype(jnp.bfloat16)


def solution(mesh):
    in_specs = (
        P(("col", "row"), None),
        P(),
        P(("row", "col"), None),
        P("row", "col", None, None),
        P("row", "col", None, None, None),
        P("row", "col", None, None, None),
    )
    out_specs = (P("row", "col", None, None, None), P(("col", "row"), None))
    step = functools.partial(local, mesh.shape["row"], mesh.shape["col"])
    return jax.shard_map(step, mesh=mesh, in_specs=in_specs, out_specs=out_specs, check_vma=False)
```

```python
import functools

import jax
import jax.numpy as jnp
from jax import lax
from jax.experimental import pallas as pl
from jax.experimental.pallas import tpu as pltpu
from jax.sharding import PartitionSpec as P

BLOCK = 128
GROUP = 8
KERNEL_VMEM = 24 << 20
VMEM = pltpu.VMEM
SMEM = pltpu.SMEM


def in_vmem(x):
    return pltpu.with_memory_space_constraint(x, VMEM)


def in_hbm(x):
    return pltpu.with_memory_space_constraint(x, pltpu.HBM)


def swap(x, axis, size, mask):
    return lax.ppermute(x, axis, [(i, i ^ mask) for i in range(size)])


def swap_rows(x, n_row, n_col, even, odd):
    places = [(r, c) for r in range(n_row) for c in range(n_col)]
    pairs = [(r * n_col + c, (r ^ (odd if c % 2 else even)) * n_col + c) for r, c in places]
    return lax.ppermute(x, ("row", "col"), pairs)


def hidden_kernel(grads, weight, out, grad_buf, weight_buf, sems):
    copies = [
        pltpu.make_async_copy(grads, grad_buf, sems.at[0]),
        pltpu.make_async_copy(weight, weight_buf, sems.at[1]),
    ]
    for copy in copies:
        copy.start()
    for copy in copies:
        copy.wait()
    out[...] = lax.dot_general(
        grad_buf[...], weight_buf[...], (((1,), (1,)), ((), ())), preferred_element_type=jnp.float32
    ).astype(out.dtype)


def prep_kernel(index, mask, weights, keep_out, adj_out, table, mask_buf, weight_buf, sems, table_sem):
    tiles = mask_buf.shape[0]
    groups = tiles // GROUP

    def fetch(g):
        span = pl.ds(pl.multiple_of(g * GROUP, GROUP), GROUP)
        return (
            pltpu.make_async_copy(mask.at[0, 0, span], mask_buf.at[span], sems.at[0, g]),
            pltpu.make_async_copy(weights.at[0, 0, span], weight_buf.at[span], sems.at[1, g]),
        )

    table_copy = pltpu.make_async_copy(index, table, table_sem)
    table_copy.start()
    for g in range(groups):
        for copy in fetch(g):
            copy.start()
    table_copy.wait()

    def body(g, carry):
        for copy in fetch(g):
            copy.wait()
        for i in range(GROUP):
            t = g * GROUP + i
            keep = (mask_buf[t] * table[0, 2, 0, t]).astype(jnp.float32).astype(jnp.bfloat16)
            keep_out[t] = keep
            adj_out[t] = (weight_buf[t] * keep).T
        return carry

    lax.fori_loop(0, groups, body, 0)


def places_kernel(n_row, n_col, per, table, places):
    tiles = table.shape[3]
    me = lax.axis_index("col")
    row = lax.axis_index("row")
    core = me % 2
    bits = n_row.bit_length() - 1

    def body(g, late):
        for i in range(GROUP):
            t = g * GROUP + i
            a = table[0, 0, 0, t]
            b = table[0, 1, 0, t]
            slot = (a // per) ^ me
            off = (b // per) ^ row
            back = sum(((off >> j) & 1) << (bits - 1 - j) for j in range(bits))
            places[t] = slot * per + a % per
            places[tiles + t] = (off + core * (back - off)) * per + b % per
            last = (slot == n_col - 1).astype(jnp.int32)
            at = (1 - last) * (t - late) + last * (tiles - 1 - late)
            late = late + last
            places[2 * tiles + at] = t
            places[3 * tiles + at] = off * per + b % per
            places[4 * tiles + at] = (1 - last) * per + last * (a % per)
        return late

    late = lax.fori_loop(0, tiles // GROUP, body, jnp.int32(0))
    places[5 * tiles] = (tiles - late) // GROUP


def sums_kernel(per, *refs):
    places, adj, *slots, panel, total = refs
    tiles = adj.shape[0]
    for s, slot in enumerate(slots):
        for i in range(per):
            panel[s * per + i] = slot[i * BLOCK : (i + 1) * BLOCK, :]
    for i in range(len(slots) * per, panel.shape[0]):
        panel[i] = jnp.zeros_like(panel[i])
    total[...] = jnp.zeros_like(total)
    for p in range(tiles):
        t = places[2 * tiles + p]
        total[places[3 * tiles + p]] += jnp.dot(adj[t], panel[places[t]], preferred_element_type=jnp.float32)


def rest_kernel(per, places, adj, total, last, *refs):
    *outs, blocks, extra = refs
    tiles = adj.shape[0]
    for i in range(per):
        blocks[i] = last[i * BLOCK : (i + 1) * BLOCK, :]
    blocks[per] = jnp.zeros_like(blocks[per])
    extra[...] = jnp.zeros_like(extra)

    def body(g, carry):
        for i in range(GROUP):
            p = g * GROUP + i
            extra[places[3 * tiles + p]] += jnp.dot(
                adj[places[2 * tiles + p]], blocks[places[4 * tiles + p]], preferred_element_type=jnp.float32
            )
        return carry

    lax.fori_loop(places[5 * tiles], tiles // GROUP, body, 0)
    for s, out in enumerate(outs):
        for i in range(per):
            found = total[s * per + i] + extra[s * per + i]
            out[i * BLOCK : (i + 1) * BLOCK, :] = found.astype(out.dtype)


def scores_kernel(per, places, panel, last, keep, features, out, rows, cols, stage, sems):
    tiles = keep.shape[0]
    head = rows.shape[0] - per
    rows[:head] = panel[:head]
    for i in range(per):
        rows[head + i] = last[i * BLOCK : (i + 1) * BLOCK, :]
    for i in range(cols.shape[0]):
        cols[i] = features[i * BLOCK : (i + 1) * BLOCK, :].T
    copies = []
    for g in range(tiles // GROUP):
        for t in range(g * GROUP, (g + 1) * GROUP):
            found = jnp.dot(rows[places[t]], cols[places[tiles + t]], preferred_element_type=jnp.float32)
            stage[t] = found.astype(jnp.bfloat16) * keep[t]
        span = pl.ds(g * GROUP, GROUP)
        copies.append(pltpu.make_async_copy(stage.at[span], out.at[0, 0, span], sems.at[g]))
        copies[-1].start()
    for copy in copies:
        copy.wait()


def local(n_row, n_col, features, weight, out_grad, tile_index, edge_mask, edge_weight):
    tiles = edge_mask.shape[2]
    nodes, fin = features.shape
    per = nodes // BLOCK
    whole = pl.BlockSpec(memory_space=VMEM)
    far = pl.BlockSpec(memory_space=pl.ANY)
    scalars = pl.BlockSpec(memory_space=SMEM)
    params = pltpu.CompilerParams(vmem_limit_bytes=KERNEL_VMEM)
    tile_set = VMEM((tiles, BLOCK, BLOCK), jnp.bfloat16)
    product_flops = 2 * tiles * BLOCK * BLOCK * fin

    hidden = pl.pallas_call(
        hidden_kernel,
        in_specs=[far, far],
        out_specs=whole,
        out_shape=VMEM((nodes, fin), jnp.bfloat16),
        scratch_shapes=[
            VMEM(out_grad.shape, out_grad.dtype),
            VMEM(weight.shape, weight.dtype),
            pltpu.SemaphoreType.DMA((2,)),
        ],
        compiler_params=params,
        name="hidden",
    )(in_hbm(out_grad), in_hbm(weight))

    masks = [1 << i for i in reversed(range(1, n_col.bit_length() - 1))]
    shards = {0: hidden}
    for mask in masks:
        shards[mask] = swap(hidden, "col", n_col, mask)
    features, hidden = lax.optimization_barrier((features, hidden))
    bits = [1 << i for i in range(n_row.bit_length() - 1)]
    stages = list(zip(bits, reversed(bits), strict=True))
    cols = [features, swap_rows(features, n_row, n_col, *stages[0])]

    index = jnp.transpose(tile_index, (0, 3, 1, 2))
    keep, adj, table = pl.pallas_call(
        prep_kernel,
        in_specs=[far, far, far],
        out_specs=[whole, whole, scalars],
        out_shape=[tile_set, tile_set, SMEM(index.shape, jnp.int32)],
        scratch_shapes=[
            VMEM((tiles, BLOCK, BLOCK), jnp.int32),
            VMEM((tiles, BLOCK, BLOCK), jnp.bfloat16),
            pltpu.SemaphoreType.DMA((2, tiles // GROUP)),
            pltpu.SemaphoreType.DMA,
        ],
        cost_estimate=pl.CostEstimate(flops=0, bytes_accessed=4096, transcendentals=0),
        compiler_params=params,
        name="prep",
    )(in_hbm(index), in_hbm(edge_mask), in_hbm(edge_weight))
    places = pl.pallas_call(
        functools.partial(places_kernel, n_row, n_col, per),
        in_specs=[scalars],
        out_specs=scalars,
        out_shape=SMEM((5 * tiles + 1,), jnp.int32),
        cost_estimate=pl.CostEstimate(flops=0, bytes_accessed=4096, transcendentals=0),
        compiler_params=params,
        name="places",
    )(pltpu.with_memory_space_constraint(table, SMEM))
    places = pltpu.with_memory_space_constraint(places, SMEM)

    shards[masks[0]], hidden, keep, adj = lax.optimization_barrier((shards[masks[0]], hidden, keep, adj))
    shards[0] = hidden
    cols, keep = lax.optimization_barrier((cols, keep))
    for i, mask in enumerate(masks[1:], 1):
        for s in range(masks[i - 1], n_col, masks[i - 1]):
            shards[s ^ mask] = swap(shards[s], "col", n_col, mask)
    cols = jnp.concatenate(cols)
    for stage in stages[1:]:
        cols = jnp.concatenate([cols, swap_rows(cols, n_row, n_col, *stage)])
    slots = [shards[s] for s in range(0, n_col, 2)]
    slots = [x for shard in slots for x in (shard, swap(shard, "col", n_col, 1))]

    *slots, last = slots
    total_shape = (n_row * per, BLOCK, fin)
    panel, total = pl.pallas_call(
        functools.partial(sums_kernel, per),
        in_specs=[scalars] + [whole] * n_col,
        out_specs=[whole] * 2,
        out_shape=[VMEM((n_col * per, BLOCK, fin), jnp.bfloat16), VMEM(total_shape, jnp.float32)],
        cost_estimate=pl.CostEstimate(flops=product_flops, bytes_accessed=1 << 20, transcendentals=0),
        compiler_params=params,
        name="sums",
    )(places, *map(in_vmem, (adj, *slots)))
    own, *parts = pl.pallas_call(
        functools.partial(rest_kernel, per),
        in_specs=[scalars] + [whole] * 3,
        out_specs=[whole] * n_row,
        out_shape=[VMEM((nodes, fin), jnp.float32)] + [VMEM((nodes, fin), jnp.bfloat16)] * (n_row - 1),
        scratch_shapes=[VMEM((per + 1, BLOCK, fin), jnp.bfloat16), VMEM(total_shape, jnp.float32)],
        cost_estimate=pl.CostEstimate(flops=0, bytes_accessed=4096, transcendentals=0),
        compiler_params=params,
        name="rest",
    )(places, *map(in_vmem, (adj, total, last)))

    order = sorted(range(1, n_row), key=lambda s: -s.bit_count())
    order = order[-1:] + order[:-1]
    got = [swap(parts[s - 1], "row", n_row, s) for s in order]

    edge_grad = pl.pallas_call(
        functools.partial(scores_kernel, per),
        in_specs=[scalars] + [whole] * 4,
        out_specs=far,
        out_shape=jax.ShapeDtypeStruct(edge_weight.shape, jnp.bfloat16),
        scratch_shapes=[
            VMEM((n_col * per, BLOCK, fin), jnp.bfloat16),
            VMEM((n_row * per, fin, BLOCK), jnp.bfloat16),
            VMEM((tiles, BLOCK, BLOCK), jnp.bfloat16),
            pltpu.SemaphoreType.DMA((tiles // GROUP,)),
        ],
        cost_estimate=pl.CostEstimate(flops=product_flops, bytes_accessed=4 << 20, transcendentals=0),
        compiler_params=params,
        name="scores",
    )(places, *map(in_vmem, (panel, last, keep, cols)))

    for part in got:
        own = own + part.astype(jnp.float32)
    return edge_grad, own.astype(jnp.bfloat16)


def solution(mesh):
    in_specs = (
        P(("col", "row"), None),
        P(),
        P(("row", "col"), None),
        P("row", "col", None, None),
        P("row", "col", None, None, None),
        P("row", "col", None, None, None),
    )
    out_specs = (P("row", "col", None, None, None), P(("col", "row"), None))
    step = functools.partial(local, mesh.shape["row"], mesh.shape["col"])
    return jax.shard_map(step, mesh=mesh, in_specs=in_specs, out_specs=out_specs, check_vma=False)
```

```python
import functools

import jax
import jax.numpy as jnp
from jax import lax
from jax.experimental import pallas as pl
from jax.experimental.pallas import tpu as pltpu
from jax.sharding import PartitionSpec as P

BLOCK = 128
GROUP = 8
KERNEL_VMEM = 24 << 20
VMEM = pltpu.VMEM
SMEM = pltpu.SMEM


def in_vmem(x):
    return pltpu.with_memory_space_constraint(x, VMEM)


def in_hbm(x):
    return pltpu.with_memory_space_constraint(x, pltpu.HBM)


def swap(x, axis, size, mask):
    return lax.ppermute(x, axis, [(i, i ^ mask) for i in range(size)])


def swap_rows(x, n_row, n_col, even, odd):
    places = [(r, c) for r in range(n_row) for c in range(n_col)]
    pairs = [(r * n_col + c, (r ^ (odd if c % 2 else even)) * n_col + c) for r, c in places]
    return lax.ppermute(x, ("row", "col"), pairs)


def hidden_kernel(grads, weight, out, grad_buf, weight_buf, sems):
    copies = [
        pltpu.make_async_copy(grads, grad_buf, sems.at[0]),
        pltpu.make_async_copy(weight, weight_buf, sems.at[1]),
    ]
    for copy in copies:
        copy.start()
    for copy in copies:
        copy.wait()
    out[...] = lax.dot_general(
        grad_buf[...], weight_buf[...], (((1,), (1,)), ((), ())), preferred_element_type=jnp.float32
    ).astype(out.dtype)


def prep_kernel(index, mask, weights, keep_out, adj_out, table, mask_buf, weight_buf, sems, table_sem):
    tiles = mask_buf.shape[0]
    groups = tiles // GROUP

    def fetch(g):
        span = pl.ds(pl.multiple_of(g * GROUP, GROUP), GROUP)
        return (
            pltpu.make_async_copy(mask.at[0, 0, span], mask_buf.at[span], sems.at[0, g]),
            pltpu.make_async_copy(weights.at[0, 0, span], weight_buf.at[span], sems.at[1, g]),
        )

    table_copy = pltpu.make_async_copy(index, table, table_sem)
    table_copy.start()
    for g in range(groups):
        for copy in fetch(g):
            copy.start()
    table_copy.wait()

    def body(g, carry):
        for copy in fetch(g):
            copy.wait()
        for i in range(GROUP):
            t = g * GROUP + i
            keep = (mask_buf[t] * table[0, 2, 0, t]).astype(jnp.float32).astype(jnp.bfloat16)
            keep_out[t] = keep
            adj_out[t] = (weight_buf[t] * keep).T
        return carry

    lax.fori_loop(0, groups, body, 0)


def places_kernel(n_row, n_col, per, table, places):
    tiles = table.shape[3]
    me = lax.axis_index("col")
    row = lax.axis_index("row")
    core = me % 2
    bits = n_row.bit_length() - 1

    def body(g, late):
        for i in range(GROUP):
            t = g * GROUP + i
            a = table[0, 0, 0, t]
            b = table[0, 1, 0, t]
            slot = (a // per) ^ me
            off = (b // per) ^ row
            back = sum(((off >> j) & 1) << (bits - 1 - j) for j in range(bits))
            places[t] = slot * per + a % per
            places[tiles + t] = (off + core * (back - off)) * per + b % per
            last = (slot == n_col - 1).astype(jnp.int32)
            at = (1 - last) * (t - late) + last * (tiles - 1 - late)
            late = late + last
            places[2 * tiles + at] = t
            places[3 * tiles + at] = off * per + b % per
            places[4 * tiles + at] = (1 - last) * per + last * (a % per)
        return late

    late = lax.fori_loop(0, tiles // GROUP, body, jnp.int32(0))
    places[5 * tiles] = (tiles - late) // GROUP


def sums_kernel(per, *refs):
    places, adj, *slots, panel, total = refs
    tiles = adj.shape[0]
    for s, slot in enumerate(slots):
        for i in range(per):
            panel[s * per + i] = slot[i * BLOCK : (i + 1) * BLOCK, :]
    for i in range(len(slots) * per, panel.shape[0]):
        panel[i] = jnp.zeros_like(panel[i])
    total[...] = jnp.zeros_like(total)
    for p in range(tiles):
        t = places[2 * tiles + p]
        total[places[3 * tiles + p]] += jnp.dot(adj[t], panel[places[t]], preferred_element_type=jnp.float32)


def rest_kernel(per, places, adj, start, last, *refs):
    total, *outs, blocks = refs
    tiles = adj.shape[0]
    for i in range(per):
        blocks[i] = last[i * BLOCK : (i + 1) * BLOCK, :]
    blocks[per] = jnp.zeros_like(blocks[per])

    def body(g, carry):
        for i in range(GROUP):
            p = g * GROUP + i
            total[places[3 * tiles + p]] += jnp.dot(
                adj[places[2 * tiles + p]], blocks[places[4 * tiles + p]], preferred_element_type=jnp.float32
            )
        return carry

    lax.fori_loop(places[5 * tiles], tiles // GROUP, body, 0)
    for s, out in enumerate(outs):
        for i in range(per):
            out[i * BLOCK : (i + 1) * BLOCK, :] = total[s * per + i].astype(out.dtype)


def scores_kernel(per, places, panel, last, keep, features, out, rows, cols, stage, sems):
    tiles = keep.shape[0]
    head = rows.shape[0] - per
    rows[:head] = panel[:head]
    for i in range(per):
        rows[head + i] = last[i * BLOCK : (i + 1) * BLOCK, :]
    for i in range(cols.shape[0]):
        cols[i] = features[i * BLOCK : (i + 1) * BLOCK, :].T
    copies = []
    for g in range(tiles // GROUP):
        for t in range(g * GROUP, (g + 1) * GROUP):
            found = jnp.dot(rows[places[t]], cols[places[tiles + t]], preferred_element_type=jnp.float32)
            stage[t] = found.astype(jnp.bfloat16) * keep[t]
        span = pl.ds(g * GROUP, GROUP)
        copies.append(pltpu.make_async_copy(stage.at[span], out.at[0, 0, span], sems.at[g]))
        copies[-1].start()
    for copy in copies:
        copy.wait()


def local(n_row, n_col, features, weight, out_grad, tile_index, edge_mask, edge_weight):
    tiles = edge_mask.shape[2]
    nodes, fin = features.shape
    per = nodes // BLOCK
    whole = pl.BlockSpec(memory_space=VMEM)
    far = pl.BlockSpec(memory_space=pl.ANY)
    scalars = pl.BlockSpec(memory_space=SMEM)
    params = pltpu.CompilerParams(vmem_limit_bytes=KERNEL_VMEM)
    tile_set = VMEM((tiles, BLOCK, BLOCK), jnp.bfloat16)
    product_flops = 2 * tiles * BLOCK * BLOCK * fin

    hidden = pl.pallas_call(
        hidden_kernel,
        in_specs=[far, far],
        out_specs=whole,
        out_shape=VMEM((nodes, fin), jnp.bfloat16),
        scratch_shapes=[
            VMEM(out_grad.shape, out_grad.dtype),
            VMEM(weight.shape, weight.dtype),
            pltpu.SemaphoreType.DMA((2,)),
        ],
        compiler_params=params,
        name="hidden",
    )(in_hbm(out_grad), in_hbm(weight))

    masks = [1 << i for i in reversed(range(1, n_col.bit_length() - 1))]
    shards = {0: hidden}
    for mask in masks:
        shards[mask] = swap(hidden, "col", n_col, mask)
    features, hidden = lax.optimization_barrier((features, hidden))
    bits = [1 << i for i in range(n_row.bit_length() - 1)]
    stages = list(zip(bits, reversed(bits), strict=True))
    cols = [features, swap_rows(features, n_row, n_col, *stages[0])]

    index = jnp.transpose(tile_index, (0, 3, 1, 2))
    keep, adj, table = pl.pallas_call(
        prep_kernel,
        in_specs=[far, far, far],
        out_specs=[whole, whole, scalars],
        out_shape=[tile_set, tile_set, SMEM(index.shape, jnp.int32)],
        scratch_shapes=[
            VMEM((tiles, BLOCK, BLOCK), jnp.int32),
            VMEM((tiles, BLOCK, BLOCK), jnp.bfloat16),
            pltpu.SemaphoreType.DMA((2, tiles // GROUP)),
            pltpu.SemaphoreType.DMA,
        ],
        cost_estimate=pl.CostEstimate(flops=0, bytes_accessed=4096, transcendentals=0),
        compiler_params=params,
        name="prep",
    )(in_hbm(index), in_hbm(edge_mask), in_hbm(edge_weight))
    places = pl.pallas_call(
        functools.partial(places_kernel, n_row, n_col, per),
        in_specs=[scalars],
        out_specs=scalars,
        out_shape=SMEM((5 * tiles + 1,), jnp.int32),
        cost_estimate=pl.CostEstimate(flops=0, bytes_accessed=4096, transcendentals=0),
        compiler_params=params,
        name="places",
    )(pltpu.with_memory_space_constraint(table, SMEM))
    places = pltpu.with_memory_space_constraint(places, SMEM)

    shards[masks[0]], hidden, keep, adj = lax.optimization_barrier((shards[masks[0]], hidden, keep, adj))
    shards[0] = hidden
    cols, keep = lax.optimization_barrier((cols, keep))
    for i, mask in enumerate(masks[1:], 1):
        for s in range(masks[i - 1], n_col, masks[i - 1]):
            shards[s ^ mask] = swap(shards[s], "col", n_col, mask)
    cols = jnp.concatenate(cols)
    for stage in stages[1:]:
        cols = jnp.concatenate([cols, swap_rows(cols, n_row, n_col, *stage)])
    slots = [shards[s] for s in range(0, n_col, 2)]
    slots = [x for shard in slots for x in (shard, swap(shard, "col", n_col, 1))]

    *slots, last = slots
    total_shape = (n_row * per, BLOCK, fin)
    panel, total = pl.pallas_call(
        functools.partial(sums_kernel, per),
        in_specs=[scalars] + [whole] * n_col,
        out_specs=[whole] * 2,
        out_shape=[VMEM((n_col * per, BLOCK, fin), jnp.bfloat16), VMEM(total_shape, jnp.float32)],
        cost_estimate=pl.CostEstimate(flops=product_flops, bytes_accessed=1 << 20, transcendentals=0),
        compiler_params=params,
        name="sums",
    )(places, *map(in_vmem, (adj, *slots)))
    _, own, *parts = pl.pallas_call(
        functools.partial(rest_kernel, per),
        in_specs=[scalars] + [whole] * 3,
        out_specs=[whole] * (1 + n_row),
        out_shape=[VMEM(total_shape, jnp.float32), VMEM((nodes, fin), jnp.float32)]
        + [VMEM((nodes, fin), jnp.bfloat16)] * (n_row - 1),
        scratch_shapes=[VMEM((per + 1, BLOCK, fin), jnp.bfloat16)],
        input_output_aliases={2: 0},
        cost_estimate=pl.CostEstimate(flops=0, bytes_accessed=4096, transcendentals=0),
        compiler_params=params,
        name="rest",
    )(places, *map(in_vmem, (adj, total, last)))

    order = sorted(range(1, n_row), key=lambda s: -s.bit_count())
    order = order[-1:] + order[:-1]
    got = [swap(parts[s - 1], "row", n_row, s) for s in order]

    edge_grad = pl.pallas_call(
        functools.partial(scores_kernel, per),
        in_specs=[scalars] + [whole] * 4,
        out_specs=far,
        out_shape=jax.ShapeDtypeStruct(edge_weight.shape, jnp.bfloat16),
        scratch_shapes=[
            VMEM((n_col * per, BLOCK, fin), jnp.bfloat16),
            VMEM((n_row * per, fin, BLOCK), jnp.bfloat16),
            VMEM((tiles, BLOCK, BLOCK), jnp.bfloat16),
            pltpu.SemaphoreType.DMA((tiles // GROUP,)),
        ],
        cost_estimate=pl.CostEstimate(flops=product_flops, bytes_accessed=4 << 20, transcendentals=0),
        compiler_params=params,
        name="scores",
    )(places, *map(in_vmem, (panel, last, keep, cols)))

    for part in got:
        own = own + part.astype(jnp.float32)
    return edge_grad, own.astype(jnp.bfloat16)


def solution(mesh):
    in_specs = (
        P(("col", "row"), None),
        P(),
        P(("row", "col"), None),
        P("row", "col", None, None),
        P("row", "col", None, None, None),
        P("row", "col", None, None, None),
    )
    out_specs = (P("row", "col", None, None, None), P(("col", "row"), None))
    step = functools.partial(local, mesh.shape["row"], mesh.shape["col"])
    return jax.shard_map(step, mesh=mesh, in_specs=in_specs, out_specs=out_specs, check_vma=False)
```

```python
import functools

import jax
import jax.numpy as jnp
from jax import lax
from jax.experimental import pallas as pl
from jax.experimental.pallas import tpu as pltpu
from jax.sharding import PartitionSpec as P

BLOCK = 128
GROUP = 8
KERNEL_VMEM = 24 << 20
VMEM = pltpu.VMEM
SMEM = pltpu.SMEM


def in_vmem(x):
    return pltpu.with_memory_space_constraint(x, VMEM)


def in_hbm(x):
    return pltpu.with_memory_space_constraint(x, pltpu.HBM)


def swap(x, axis, size, mask):
    return lax.ppermute(x, axis, [(i, i ^ mask) for i in range(size)])


def swap_rows(x, n_row, n_col, even, odd):
    places = [(r, c) for r in range(n_row) for c in range(n_col)]
    pairs = [(r * n_col + c, (r ^ (odd if c % 2 else even)) * n_col + c) for r, c in places]
    return lax.ppermute(x, ("row", "col"), pairs)


def hidden_kernel(grads, weight, out, grad_buf, weight_buf, sems):
    copies = [
        pltpu.make_async_copy(grads, grad_buf, sems.at[0]),
        pltpu.make_async_copy(weight, weight_buf, sems.at[1]),
    ]
    for copy in copies:
        copy.start()
    for copy in copies:
        copy.wait()
    out[...] = lax.dot_general(
        grad_buf[...], weight_buf[...], (((1,), (1,)), ((), ())), preferred_element_type=jnp.float32
    ).astype(out.dtype)


def prep_kernel(index, mask, weights, keep_out, adj_out, table, mask_buf, weight_buf, sems, table_sem):
    tiles = mask_buf.shape[0]
    groups = tiles // GROUP

    def fetch(g):
        span = pl.ds(pl.multiple_of(g * GROUP, GROUP), GROUP)
        return (
            pltpu.make_async_copy(mask.at[0, 0, span], mask_buf.at[span], sems.at[0, g]),
            pltpu.make_async_copy(weights.at[0, 0, span], weight_buf.at[span], sems.at[1, g]),
        )

    table_copy = pltpu.make_async_copy(index, table, table_sem)
    table_copy.start()
    for g in range(groups):
        for copy in fetch(g):
            copy.start()
    table_copy.wait()

    def body(g, carry):
        for copy in fetch(g):
            copy.wait()
        for i in range(GROUP):
            t = g * GROUP + i
            keep = (mask_buf[t] * table[0, 2, 0, t]).astype(jnp.float32).astype(jnp.bfloat16)
            keep_out[t] = keep
            adj_out[t] = (weight_buf[t] * keep).T
        return carry

    lax.fori_loop(0, groups, body, 0)


def places_kernel(n_row, n_col, per, table, places):
    tiles = table.shape[3]
    me = lax.axis_index("col")
    row = lax.axis_index("row")
    core = me % 2
    bits = n_row.bit_length() - 1

    def body(g, late):
        for i in range(GROUP):
            t = g * GROUP + i
            a = table[0, 0, 0, t]
            b = table[0, 1, 0, t]
            slot = (a // per) ^ me
            off = (b // per) ^ row
            back = sum(((off >> j) & 1) << (bits - 1 - j) for j in range(bits))
            places[t] = slot * per + a % per
            places[tiles + t] = (off + core * (back - off)) * per + b % per
            last = (slot == n_col - 1).astype(jnp.int32)
            at = (1 - last) * (t - late) + last * (tiles - 1 - late)
            late = late + last
            places[2 * tiles + at] = t
            places[3 * tiles + at] = off * per + b % per
            places[4 * tiles + at] = (1 - last) * per + last * (a % per)
        return late

    late = lax.fori_loop(0, tiles // GROUP, body, jnp.int32(0))
    places[5 * tiles] = (tiles - late) // GROUP


def sums_kernel(per, *refs):
    places, adj, *slots, panel, total = refs
    tiles = adj.shape[0]
    for s, slot in enumerate(slots):
        for i in range(per):
            panel[s * per + i] = slot[i * BLOCK : (i + 1) * BLOCK, :]
    for i in range(len(slots) * per, panel.shape[0]):
        panel[i] = jnp.zeros_like(panel[i])
    total[...] = jnp.zeros_like(total)
    for p in range(tiles):
        t = places[2 * tiles + p]
        total[places[3 * tiles + p]] += jnp.dot(adj[t], panel[places[t]], preferred_element_type=jnp.float32)


def rest_kernel(per, pairs, places, adj, start, last, *refs):
    total, *outs, blocks = refs
    tiles = adj.shape[0]
    for i in range(per):
        blocks[i] = last[i * BLOCK : (i + 1) * BLOCK, :]
    blocks[per] = jnp.zeros_like(blocks[per])

    def body(g, carry):
        for i in range(GROUP):
            p = g * GROUP + i
            total[places[3 * tiles + p]] += jnp.dot(
                adj[places[2 * tiles + p]], blocks[places[4 * tiles + p]], preferred_element_type=jnp.float32
            )
        return carry

    lax.fori_loop(places[5 * tiles], tiles // GROUP, body, 0)
    core = lax.axis_index("col") % 2
    for (even, odd), out in zip(pairs, outs, strict=True):
        chunk = (even + core * (odd - even)) * per
        for i in range(per):
            out[i * BLOCK : (i + 1) * BLOCK, :] = total[chunk + i].astype(out.dtype)


def scores_kernel(per, places, panel, last, keep, features, out, rows, cols, stage, sems):
    tiles = keep.shape[0]
    head = rows.shape[0] - per
    rows[:head] = panel[:head]
    for i in range(per):
        rows[head + i] = last[i * BLOCK : (i + 1) * BLOCK, :]
    for i in range(cols.shape[0]):
        cols[i] = features[i * BLOCK : (i + 1) * BLOCK, :].T
    copies = []
    for g in range(tiles // GROUP):
        for t in range(g * GROUP, (g + 1) * GROUP):
            found = jnp.dot(rows[places[t]], cols[places[tiles + t]], preferred_element_type=jnp.float32)
            stage[t] = found.astype(jnp.bfloat16) * keep[t]
        span = pl.ds(g * GROUP, GROUP)
        copies.append(pltpu.make_async_copy(stage.at[span], out.at[0, 0, span], sems.at[g]))
        copies[-1].start()
    for copy in copies:
        copy.wait()


def local(n_row, n_col, features, weight, out_grad, tile_index, edge_mask, edge_weight):
    tiles = edge_mask.shape[2]
    nodes, fin = features.shape
    per = nodes // BLOCK
    whole = pl.BlockSpec(memory_space=VMEM)
    far = pl.BlockSpec(memory_space=pl.ANY)
    scalars = pl.BlockSpec(memory_space=SMEM)
    params = pltpu.CompilerParams(vmem_limit_bytes=KERNEL_VMEM)
    tile_set = VMEM((tiles, BLOCK, BLOCK), jnp.bfloat16)
    product_flops = 2 * tiles * BLOCK * BLOCK * fin

    hidden = pl.pallas_call(
        hidden_kernel,
        in_specs=[far, far],
        out_specs=whole,
        out_shape=VMEM((nodes, fin), jnp.bfloat16),
        scratch_shapes=[
            VMEM(out_grad.shape, out_grad.dtype),
            VMEM(weight.shape, weight.dtype),
            pltpu.SemaphoreType.DMA((2,)),
        ],
        compiler_params=params,
        name="hidden",
    )(in_hbm(out_grad), in_hbm(weight))

    masks = [1 << i for i in reversed(range(1, n_col.bit_length() - 1))]
    shards = {0: hidden}
    for mask in masks:
        shards[mask] = swap(hidden, "col", n_col, mask)
    features, hidden = lax.optimization_barrier((features, hidden))
    bits = [1 << i for i in range(n_row.bit_length() - 1)]
    stages = list(zip(bits, reversed(bits), strict=True))
    cols = [features, swap_rows(features, n_row, n_col, *stages[0])]

    index = jnp.transpose(tile_index, (0, 3, 1, 2))
    keep, adj, table = pl.pallas_call(
        prep_kernel,
        in_specs=[far, far, far],
        out_specs=[whole, whole, scalars],
        out_shape=[tile_set, tile_set, SMEM(index.shape, jnp.int32)],
        scratch_shapes=[
            VMEM((tiles, BLOCK, BLOCK), jnp.int32),
            VMEM((tiles, BLOCK, BLOCK), jnp.bfloat16),
            pltpu.SemaphoreType.DMA((2, tiles // GROUP)),
            pltpu.SemaphoreType.DMA,
        ],
        cost_estimate=pl.CostEstimate(flops=0, bytes_accessed=4096, transcendentals=0),
        compiler_params=params,
        name="prep",
    )(in_hbm(index), in_hbm(edge_mask), in_hbm(edge_weight))
    places = pl.pallas_call(
        functools.partial(places_kernel, n_row, n_col, per),
        in_specs=[scalars],
        out_specs=scalars,
        out_shape=SMEM((5 * tiles + 1,), jnp.int32),
        cost_estimate=pl.CostEstimate(flops=0, bytes_accessed=4096, transcendentals=0),
        compiler_params=params,
        name="places",
    )(pltpu.with_memory_space_constraint(table, SMEM))
    places = pltpu.with_memory_space_constraint(places, SMEM)

    shards[masks[0]], hidden, keep, adj = lax.optimization_barrier((shards[masks[0]], hidden, keep, adj))
    shards[0] = hidden
    cols, keep = lax.optimization_barrier((cols, keep))
    for i, mask in enumerate(masks[1:], 1):
        for s in range(masks[i - 1], n_col, masks[i - 1]):
            shards[s ^ mask] = swap(shards[s], "col", n_col, mask)
    cols = jnp.concatenate(cols)
    for stage in stages[1:]:
        cols = jnp.concatenate([cols, swap_rows(cols, n_row, n_col, *stage)])
    slots = [shards[s] for s in range(0, n_col, 2)]
    slots = [x for shard in slots for x in (shard, swap(shard, "col", n_col, 1))]

    *slots, last = slots
    total_shape = (n_row * per, BLOCK, fin)
    panel, total = pl.pallas_call(
        functools.partial(sums_kernel, per),
        in_specs=[scalars] + [whole] * n_col,
        out_specs=[whole] * 2,
        out_shape=[VMEM((n_col * per, BLOCK, fin), jnp.bfloat16), VMEM(total_shape, jnp.float32)],
        cost_estimate=pl.CostEstimate(flops=product_flops, bytes_accessed=1 << 20, transcendentals=0),
        compiler_params=params,
        name="sums",
    )(places, *map(in_vmem, (adj, *slots)))
    if n_row == 4:
        pairs = [(3, 3), (1, 2), (2, 1)]
    else:
        pairs = [(s, s) for s in sorted(range(1, n_row), key=lambda s: -s.bit_count())]
    pairs = pairs[-1:] + pairs[:-1]
    _, own, *parts = pl.pallas_call(
        functools.partial(rest_kernel, per, [(0, 0)] + pairs),
        in_specs=[scalars] + [whole] * 3,
        out_specs=[whole] * (1 + n_row),
        out_shape=[VMEM(total_shape, jnp.float32), VMEM((nodes, fin), jnp.float32)]
        + [VMEM((nodes, fin), jnp.bfloat16)] * (n_row - 1),
        scratch_shapes=[VMEM((per + 1, BLOCK, fin), jnp.bfloat16)],
        input_output_aliases={2: 0},
        cost_estimate=pl.CostEstimate(flops=0, bytes_accessed=4096, transcendentals=0),
        compiler_params=params,
        name="rest",
    )(places, *map(in_vmem, (adj, total, last)))

    got = [swap_rows(x, n_row, n_col, *pair) for x, pair in zip(parts, pairs, strict=True)]

    edge_grad = pl.pallas_call(
        functools.partial(scores_kernel, per),
        in_specs=[scalars] + [whole] * 4,
        out_specs=far,
        out_shape=jax.ShapeDtypeStruct(edge_weight.shape, jnp.bfloat16),
        scratch_shapes=[
            VMEM((n_col * per, BLOCK, fin), jnp.bfloat16),
            VMEM((n_row * per, fin, BLOCK), jnp.bfloat16),
            VMEM((tiles, BLOCK, BLOCK), jnp.bfloat16),
            pltpu.SemaphoreType.DMA((tiles // GROUP,)),
        ],
        cost_estimate=pl.CostEstimate(flops=product_flops, bytes_accessed=4 << 20, transcendentals=0),
        compiler_params=params,
        name="scores",
    )(places, *map(in_vmem, (panel, last, keep, cols)))

    for part in got:
        own = own + part.astype(jnp.float32)
    return edge_grad, own.astype(jnp.bfloat16)


def solution(mesh):
    in_specs = (
        P(("col", "row"), None),
        P(),
        P(("row", "col"), None),
        P("row", "col", None, None),
        P("row", "col", None, None, None),
        P("row", "col", None, None, None),
    )
    out_specs = (P("row", "col", None, None, None), P(("col", "row"), None))
    step = functools.partial(local, mesh.shape["row"], mesh.shape["col"])
    return jax.shard_map(step, mesh=mesh, in_specs=in_specs, out_specs=out_specs, check_vma=False)
```

```python
import functools

import jax
import jax.numpy as jnp
from jax import lax
from jax.experimental import pallas as pl
from jax.experimental.pallas import tpu as pltpu
from jax.sharding import PartitionSpec as P

BLOCK = 128
GROUP = 8
KERNEL_VMEM = 24 << 20
VMEM = pltpu.VMEM
SMEM = pltpu.SMEM


def in_vmem(x):
    return pltpu.with_memory_space_constraint(x, VMEM)


def in_hbm(x):
    return pltpu.with_memory_space_constraint(x, pltpu.HBM)


def swap(x, axis, size, mask):
    return lax.ppermute(x, axis, [(i, i ^ mask) for i in range(size)])


def swap_rows(x, n_row, n_col, even, odd):
    places = [(r, c) for r in range(n_row) for c in range(n_col)]
    pairs = [(r * n_col + c, (r ^ (odd if c % 2 else even)) * n_col + c) for r, c in places]
    return lax.ppermute(x, ("row", "col"), pairs)


def hidden_kernel(grads, weight, out, grad_buf, weight_buf, sems):
    copies = [
        pltpu.make_async_copy(grads, grad_buf, sems.at[0]),
        pltpu.make_async_copy(weight, weight_buf, sems.at[1]),
    ]
    for copy in copies:
        copy.start()
    for copy in copies:
        copy.wait()
    out[...] = lax.dot_general(
        grad_buf[...], weight_buf[...], (((1,), (1,)), ((), ())), preferred_element_type=jnp.float32
    ).astype(out.dtype)


def prep_kernel(index, mask, weights, keep_out, adj_out, table, mask_buf, weight_buf, sems, table_sem):
    tiles = mask_buf.shape[0]
    groups = tiles // GROUP

    def fetch(g):
        span = pl.ds(pl.multiple_of(g * GROUP, GROUP), GROUP)
        return (
            pltpu.make_async_copy(mask.at[0, 0, span], mask_buf.at[span], sems.at[0, g]),
            pltpu.make_async_copy(weights.at[0, 0, span], weight_buf.at[span], sems.at[1, g]),
        )

    table_copy = pltpu.make_async_copy(index, table, table_sem)
    table_copy.start()
    for g in range(groups):
        for copy in fetch(g):
            copy.start()
    table_copy.wait()

    def body(g, carry):
        for copy in fetch(g):
            copy.wait()
        for i in range(GROUP):
            t = g * GROUP + i
            keep = (mask_buf[t] * table[0, 2, 0, t]).astype(jnp.float32).astype(jnp.bfloat16)
            keep_out[t] = keep
            adj_out[t] = (weight_buf[t] * keep).T
        return carry

    lax.fori_loop(0, groups, body, 0)


def places_kernel(n_row, n_col, per, table, places):
    tiles = table.shape[3]
    me = lax.axis_index("col")
    row = lax.axis_index("row")
    core = me % 2
    bits = n_row.bit_length() - 1

    def body(g, late):
        for i in range(GROUP):
            t = g * GROUP + i
            a = table[0, 0, 0, t]
            b = table[0, 1, 0, t]
            slot = (a // per) ^ me
            off = (b // per) ^ row
            back = sum(((off >> j) & 1) << (bits - 1 - j) for j in range(bits))
            places[t] = slot * per + a % per
            places[tiles + t] = (off + core * (back - off)) * per + b % per
            last = (slot == n_col - 1).astype(jnp.int32)
            at = (1 - last) * (t - late) + last * (tiles - 1 - late)
            late = late + last
            places[2 * tiles + at] = t
            places[3 * tiles + at] = off * per + b % per
            places[4 * tiles + at] = (1 - last) * per + last * (a % per)
        return late

    late = lax.fori_loop(0, tiles // GROUP, body, jnp.int32(0))
    places[5 * tiles] = (tiles - late) // GROUP


def sums_kernel(per, *refs):
    places, adj, *slots, panel, total = refs
    tiles = adj.shape[0]
    for s, slot in enumerate(slots):
        for i in range(per):
            panel[s * per + i] = slot[i * BLOCK : (i + 1) * BLOCK, :]
    for i in range(len(slots) * per, panel.shape[0]):
        panel[i] = jnp.zeros_like(panel[i])
    total[...] = jnp.zeros_like(total)
    for p in range(tiles):
        t = places[2 * tiles + p]
        total[places[3 * tiles + p]] += jnp.dot(adj[t], panel[places[t]], preferred_element_type=jnp.float32)


def rest_kernel(per, pairs, places, adj, start, last, *refs):
    total, *outs, blocks = refs
    tiles = adj.shape[0]
    for i in range(per):
        blocks[i] = last[i * BLOCK : (i + 1) * BLOCK, :]
    blocks[per] = jnp.zeros_like(blocks[per])

    def body(g, carry):
        for i in range(GROUP):
            p = g * GROUP + i
            total[places[3 * tiles + p]] += jnp.dot(
                adj[places[2 * tiles + p]], blocks[places[4 * tiles + p]], preferred_element_type=jnp.float32
            )
        return carry

    lax.fori_loop(places[5 * tiles], tiles // GROUP, body, 0)
    core = lax.axis_index("col") % 2
    for (even, odd), out in zip(pairs, outs, strict=True):
        chunk = (even + core * (odd - even)) * per
        for i in range(per):
            out[i * BLOCK : (i + 1) * BLOCK, :] = total[chunk + i].astype(out.dtype)


def scores_kernel(per, places, panel, last, keep, features, out, rows, cols, stage, sems):
    tiles = keep.shape[0]
    head = rows.shape[0] - per
    rows[:head] = panel[:head]
    for i in range(per):
        rows[head + i] = last[i * BLOCK : (i + 1) * BLOCK, :]
    for i in range(cols.shape[0]):
        cols[i] = features[i * BLOCK : (i + 1) * BLOCK, :].T
    copies = []
    for g in range(tiles // GROUP):
        for t in range(g * GROUP, (g + 1) * GROUP):
            found = jnp.dot(rows[places[t]], cols[places[tiles + t]], preferred_element_type=jnp.float32)
            stage[t] = found.astype(jnp.bfloat16) * keep[t]
        span = pl.ds(g * GROUP, GROUP)
        copies.append(pltpu.make_async_copy(stage.at[span], out.at[0, 0, span], sems.at[g]))
        copies[-1].start()
    for copy in copies:
        copy.wait()


def local(n_row, n_col, features, weight, out_grad, tile_index, edge_mask, edge_weight):
    tiles = edge_mask.shape[2]
    nodes, fin = features.shape
    per = nodes // BLOCK
    whole = pl.BlockSpec(memory_space=VMEM)
    far = pl.BlockSpec(memory_space=pl.ANY)
    scalars = pl.BlockSpec(memory_space=SMEM)
    params = pltpu.CompilerParams(vmem_limit_bytes=KERNEL_VMEM)
    tile_set = VMEM((tiles, BLOCK, BLOCK), jnp.bfloat16)
    product_flops = 2 * tiles * BLOCK * BLOCK * fin

    hidden = pl.pallas_call(
        hidden_kernel,
        in_specs=[far, far],
        out_specs=whole,
        out_shape=VMEM((nodes, fin), jnp.bfloat16),
        scratch_shapes=[
            VMEM(out_grad.shape, out_grad.dtype),
            VMEM(weight.shape, weight.dtype),
            pltpu.SemaphoreType.DMA((2,)),
        ],
        compiler_params=params,
        name="hidden",
    )(in_hbm(out_grad), in_hbm(weight))

    masks = [1 << i for i in reversed(range(1, n_col.bit_length() - 1))]
    shards = {0: hidden}
    for mask in masks:
        shards[mask] = swap(hidden, "col", n_col, mask)
    features, hidden = lax.optimization_barrier((features, hidden))
    bits = [1 << i for i in range(n_row.bit_length() - 1)]
    stages = list(zip(bits, reversed(bits), strict=True))
    cols = [features, swap_rows(features, n_row, n_col, *stages[0])]

    index = jnp.transpose(tile_index, (0, 3, 1, 2))
    keep, adj, table = pl.pallas_call(
        prep_kernel,
        in_specs=[far, far, far],
        out_specs=[whole, whole, scalars],
        out_shape=[tile_set, tile_set, SMEM(index.shape, jnp.int32)],
        scratch_shapes=[
            VMEM((tiles, BLOCK, BLOCK), jnp.int32),
            VMEM((tiles, BLOCK, BLOCK), jnp.bfloat16),
            pltpu.SemaphoreType.DMA((2, tiles // GROUP)),
            pltpu.SemaphoreType.DMA,
        ],
        cost_estimate=pl.CostEstimate(flops=0, bytes_accessed=4096, transcendentals=0),
        compiler_params=params,
        name="prep",
    )(in_hbm(index), in_hbm(edge_mask), in_hbm(edge_weight))
    places = pl.pallas_call(
        functools.partial(places_kernel, n_row, n_col, per),
        in_specs=[scalars],
        out_specs=scalars,
        out_shape=SMEM((5 * tiles + 1,), jnp.int32),
        cost_estimate=pl.CostEstimate(flops=0, bytes_accessed=4096, transcendentals=0),
        compiler_params=params,
        name="places",
    )(pltpu.with_memory_space_constraint(table, SMEM))
    places = pltpu.with_memory_space_constraint(places, SMEM)

    shards[masks[0]], hidden, keep, adj = lax.optimization_barrier((shards[masks[0]], hidden, keep, adj))
    shards[0] = hidden
    cols, keep = lax.optimization_barrier((cols, keep))
    for i, mask in enumerate(masks[1:], 1):
        for s in range(masks[i - 1], n_col, masks[i - 1]):
            shards[s ^ mask] = swap(shards[s], "col", n_col, mask)
    cols = jnp.concatenate(cols)
    for stage in stages[1:]:
        cols = jnp.concatenate([cols, swap_rows(cols, n_row, n_col, *stage)])
    slots = [shards[s] for s in range(0, n_col, 2)]
    slots = [x for shard in slots for x in (shard, swap(shard, "col", n_col, 1))]

    *slots, last = slots
    total_shape = (n_row * per, BLOCK, fin)
    panel, total = pl.pallas_call(
        functools.partial(sums_kernel, per),
        in_specs=[scalars] + [whole] * n_col,
        out_specs=[whole] * 2,
        out_shape=[VMEM((n_col * per, BLOCK, fin), jnp.bfloat16), VMEM(total_shape, jnp.float32)],
        cost_estimate=pl.CostEstimate(flops=product_flops, bytes_accessed=1 << 20, transcendentals=0),
        compiler_params=params,
        name="sums",
    )(places, *map(in_vmem, (adj, *slots)))
    if n_row == 4:
        pairs = [(3, 3), (1, 2), (2, 1)]
    else:
        pairs = [(s, s) for s in sorted(range(1, n_row), key=lambda s: -s.bit_count())]
    pairs = pairs[-1:] + pairs[:-1]
    total, *parts = pl.pallas_call(
        functools.partial(rest_kernel, per, pairs),
        in_specs=[scalars] + [whole] * 3,
        out_specs=[whole] * n_row,
        out_shape=[VMEM(total_shape, jnp.float32)]
        + [VMEM((nodes, fin), jnp.bfloat16)] * (n_row - 1),
        scratch_shapes=[VMEM((per + 1, BLOCK, fin), jnp.bfloat16)],
        input_output_aliases={2: 0},
        cost_estimate=pl.CostEstimate(flops=0, bytes_accessed=4096, transcendentals=0),
        compiler_params=params,
        name="rest",
    )(places, *map(in_vmem, (adj, total, last)))

    got = [swap_rows(x, n_row, n_col, *pair) for x, pair in zip(parts, pairs, strict=True)]

    edge_grad = pl.pallas_call(
        functools.partial(scores_kernel, per),
        in_specs=[scalars] + [whole] * 4,
        out_specs=far,
        out_shape=jax.ShapeDtypeStruct(edge_weight.shape, jnp.bfloat16),
        scratch_shapes=[
            VMEM((n_col * per, BLOCK, fin), jnp.bfloat16),
            VMEM((n_row * per, fin, BLOCK), jnp.bfloat16),
            VMEM((tiles, BLOCK, BLOCK), jnp.bfloat16),
            pltpu.SemaphoreType.DMA((tiles // GROUP,)),
        ],
        cost_estimate=pl.CostEstimate(flops=product_flops, bytes_accessed=4 << 20, transcendentals=0),
        compiler_params=params,
        name="scores",
    )(places, *map(in_vmem, (panel, last, keep, cols)))

    own = total[:per].reshape(nodes, fin)
    for part in got:
        own = own + part.astype(jnp.float32)
    return edge_grad, own.astype(jnp.bfloat16)


def solution(mesh):
    in_specs = (
        P(("col", "row"), None),
        P(),
        P(("row", "col"), None),
        P("row", "col", None, None),
        P("row", "col", None, None, None),
        P("row", "col", None, None, None),
    )
    out_specs = (P("row", "col", None, None, None), P(("col", "row"), None))
    step = functools.partial(local, mesh.shape["row"], mesh.shape["col"])
    return jax.shard_map(step, mesh=mesh, in_specs=in_specs, out_specs=out_specs, check_vma=False)
```
